256 devices in a mesh: cells: 128 (over x, z, y), harm: 2 (over core).
Axes of the slice: x: 4, y: 4, z: 8, core: 2. Of those that a mesh axis runs over, the one named last changes fastest.
Arguments:
- source: float32 [14, 4, 8192, 128], P('harm', None, 'cells'), may hold values from -6 to 6
- mode_shapes: bfloat16 [60, 8192, 128], P(None, 'cells'), may hold values from -5.4 to 5.4
- modal_real: float32 [7, 60, 60], replicated, may hold values from -2 to 9
- modal_imag: float32 [7, 60, 60], replicated, may hold values from -1 to 3
- harmonic_freq: float32 [7], replicated, may hold values from 0.2 to 1.5
- blade_of_row: int32 [8192], P('cells'), may hold values from 0 to 23, as said below
Outputs:
- wall_sensitivity: float32 [8192, 128], P(('cells', 'harm'))
- blade_load: float32 [24], replicated
The draws below stay inside these ranges and needn't reach their ends.
Inputs may be any that keep to these rules, and one draw needn't show every extreme that they name: `blade_of_row`: never falls along the stations; every blade owns at least 170 consecutive stations.
All inputs are finite; a program needn't handle non-finite values.
Results may differ from the reference program's by a relative error of at most 0.0049.
Values sent between devices are 32-bit elements; how exact they have to be, the bound alone decides.
A program may use at most 64 MiB of HBM per device.

```python
import math
import jax
import jax.numpy as jnp
from jax import lax

MODES = 60
HARM = 7
BLADES = 24
CHORD = 128
LAYERS = 4
STEPS = 3
COMPS = 14
NROWS = 8192


def draw_mode_shapes(key, part):
    key = jax.random.fold_in(key, 11)
    key_rough = jax.random.fold_in(key, 0)
    stations = jnp.arange(NROWS, dtype=jnp.float32)
    rising = 1.0 + 2.0 * stations / NROWS
    base = jnp.clip(jax.random.normal(key_rough, (MODES, NROWS, CHORD), jnp.float32), -6.0, 6.0)
    return (0.3 * base * rising[None, :, None]).astype(jnp.bfloat16)


def draw_modal_real(key, part):
    key = jax.random.fold_in(key, 21)
    key_off, key_diag = jax.random.split(key)
    identity = jnp.eye(MODES, dtype=jnp.float32)
    raw = jax.random.uniform(key_off, (HARM, MODES, MODES), jnp.float32, -2.0, 2.0)
    twisted = 0.5 * (raw - jnp.swapaxes(raw, 1, 2))
    diagonal = jax.random.uniform(key_diag, (HARM, MODES, 1), jnp.float32, 6.0, 9.0)
    return twisted * (1.0 - identity) + identity * diagonal


def draw_modal_imag(key, part):
    key = jax.random.fold_in(key, 22)
    key_off, key_diag = jax.random.split(key)
    identity = jnp.eye(MODES, dtype=jnp.float32)
    raw = jax.random.uniform(key_off, (HARM, MODES, MODES), jnp.float32, -1.0, 1.0)
    mirrored = 0.5 * (raw + jnp.swapaxes(raw, 1, 2))
    diagonal = jax.random.uniform(key_diag, (HARM, MODES, 1), jnp.float32, 0.5, 3.0)
    return mirrored * (1.0 - identity) + identity * diagonal


def draw_blade_of_row(key, part):
    key = jax.random.fold_in(key, 31)
    reach = NROWS // 96
    offsets = jax.random.randint(key, (BLADES - 1,), -reach, reach + 1, dtype=jnp.int32)
    cuts = jnp.arange(1, BLADES, dtype=jnp.int32) * NROWS // BLADES + offsets
    stations = jnp.arange(NROWS, dtype=jnp.int32)
    return jnp.sum((stations[:, None] >= cuts[None, :]).astype(jnp.int32), axis=1).astype(jnp.int32)


def steps_of(stream_key, extent, cuts, smallest, largest):
    level, own = 1.0, jax.random.fold_in(stream_key, 6)
    for dim, parts in cuts:
        draws = jnp.exp(jax.random.uniform(jax.random.fold_in(own, dim), (parts,), jnp.float32, smallest / len(cuts), largest / len(cuts)))
        level = level * jnp.repeat(draws, extent[dim] // parts).reshape([-1 if axis == dim else 1 for axis in range(len(extent))])
    return level


def noise(stream_key, dims, width, most, pieces=(), held_as=jnp.bfloat16):
    level = steps_of(stream_key, dims, pieces, -0.22, 0.18) if pieces else 1.0
    drawn = jax.random.normal(stream_key, dims, jnp.float32) * width * level
    return jnp.minimum(jnp.maximum(drawn, -most), most).astype(held_as)


def setup_inputs(seed: int = 0) -> dict:
    key_list = jax.random.split(jax.random.key(seed), 7)
    return {
        "source": noise(key_list[0], (COMPS, LAYERS, NROWS, CHORD), 1.0, 6.0, ((0, 2), (2, 128)), jnp.float32),
        "mode_shapes": draw_mode_shapes(jax.random.fold_in(key_list[6], 71), 0),
        "modal_real": draw_modal_real(jax.random.fold_in(key_list[6], 71), 0),
        "modal_imag": draw_modal_imag(jax.random.fold_in(key_list[6], 71), 0),
        "harmonic_freq": jnp.clip(jnp.exp(jax.random.uniform(key_list[4], (HARM,), jnp.float32, math.log(0.2), math.log(1.5))), 0.2, 1.5),
        "blade_of_row": draw_blade_of_row(jax.random.fold_in(key_list[6], 71), 0),
    }


RELAX = 0.15
DAMPING = 0.5

def advance(center, upper, lower, partner_field, forcing, coupling):
    zero_chord = jnp.zeros_like(center[..., :1])
    right = jnp.concatenate([center[..., 1:], zero_chord], axis=-1)
    left = jnp.concatenate([zero_chord, center[..., :-1]], axis=-1)
    zero_layer = jnp.zeros_like(center[:, :1])
    deeper = jnp.concatenate([center[:, 1:], zero_layer], axis=1)
    higher = jnp.concatenate([zero_layer, center[:, :-1]], axis=1)
    laplace = upper + lower + right + left + deeper + higher - 6.0 * center
    return center + RELAX * (laplace - DAMPING * center + coupling[:, None, None, None] * partner_field + forcing)

def modal_solve(load, modal_real, modal_imag):
    harm_count = modal_real.shape[0]
    mode_count = modal_real.shape[1]
    top_rows = jnp.concatenate([modal_real, -modal_imag], axis=2)
    low_rows = jnp.concatenate([modal_imag, modal_real], axis=2)
    system = jnp.concatenate([top_rows, low_rows], axis=1)
    rhs = jnp.concatenate([load[:harm_count], load[harm_count:]], axis=1)
    normal = jnp.einsum('hji,hjk->hik', system, system, precision=lax.Precision.HIGHEST)
    moved = jnp.einsum('hji,hj->hi', system, rhs, precision=lax.Precision.HIGHEST)
    factor = jnp.linalg.cholesky(normal)
    solved = jax.vmap(lambda factor_one, vector_one: jax.scipy.linalg.cho_solve((factor_one, True), vector_one))(factor, moved)
    return jnp.concatenate([solved[:, :mode_count], solved[:, mode_count:]], axis=0)

def reference(source, mode_shapes, modal_real, modal_imag, harmonic_freq, blade_of_row):
    harm_count = harmonic_freq.shape[0]
    coupling = jnp.concatenate([harmonic_freq, -harmonic_freq])
    field = source
    for step_index in range(STEPS):
        partner_field = jnp.concatenate([field[harm_count:], field[:harm_count]], axis=0)
        field = advance(field, jnp.roll(field, -1, axis=2), jnp.roll(field, 1, axis=2), partner_field, source, coupling)
    wall = field[:, 0].astype(jnp.bfloat16)
    flat_wall = wall.reshape(2 * harm_count, -1)
    shapes = mode_shapes.reshape(mode_shapes.shape[0], -1)
    face_count = flat_wall.shape[1]
    load = jnp.dot(flat_wall.astype(jnp.float32), shapes.T.astype(jnp.float32), preferred_element_type=jnp.float32) * jnp.float32(1.0 / math.sqrt(face_count))
    amplitudes = modal_solve(load, modal_real, modal_imag).astype(jnp.bfloat16)
    rebuilt = jnp.dot(amplitudes.astype(jnp.float32), shapes.astype(jnp.float32), preferred_element_type=jnp.float32)
    sensitivity = lax.optimization_barrier(jnp.sum(flat_wall.astype(jnp.float32) * rebuilt, axis=0)).reshape(NROWS, CHORD)
    onehot = (blade_of_row[None, :] == jnp.arange(BLADES, dtype=jnp.int32)[:, None]).astype(jnp.float32)
    totals = jnp.dot(onehot, lax.optimization_barrier(jnp.sum(sensitivity, axis=1)), precision=lax.Precision.HIGHEST)
    counts = lax.optimization_barrier(jnp.sum(onehot, axis=1)) * CHORD
    return (sensitivity, totals * lax.rsqrt(counts))
```

```python
import itertools

import jax
import jax.numpy as jnp
from jax import lax
from jax.experimental import pallas as pl
from jax.experimental.pallas import tpu as pltpu
from jax.sharding import PartitionSpec as P

BLADES = 24
RELAX = 0.15
DAMPING = 0.5
CENTER = 1.0 - 6.0 * RELAX - RELAX * DAMPING

HARM = 7
MODES = 60
LAYERS = 4
CHORD = 128
OWN = 32
ROWS = 48
FIRST = 5
SPAN = 38
XN, ZN, YN = 4, 8, 4
MESH = pl.DeviceIdType.MESH
HIGHEST = lax.Precision.HIGHEST


def place():
    cell = lax.axis_index("cells")
    return cell // (ZN * YN), (cell // YN) % ZN, cell % YN, lax.axis_index("harm")


def cell_of(x, z, y):
    return (x * ZN + z) * YN + y


def kernel(
    freq_ref, blade_ref, source_ref, shapes_ref, real_ref, imag_ref,
    sens_ref, load_ref,
    stage, shapes_raw, shapes_wide, shapes_flat, first, second, third, wall, wall_low,
    pair, gauss, inverse, packed, send1, recv1, send2, recv2, send3, recv3,
    local_sem, send_sem, recv_sem,
):
    x, z, y, h = place()
    cell = lax.axis_index("cells")
    cells = XN * ZN * YN
    member = y * 2 + h
    plane = x * ZN + z
    up_cell = lax.rem(cell + 1, cells)
    down_cell = lax.rem(cell + cells - 1, cells)
    mine = jnp.minimum(member, HARM - 1)

    start = h * 29
    own_row = 8 - 3 * h
    own_copy = pltpu.make_async_copy(
        source_ref.at[:, :, pl.ds(start, 35), :],
        stage.at[pl.ds(h * 8, HARM), :, pl.ds(own_row, 35), :],
        local_sem.at[0],
    )
    own_copy.start()
    shape_copy = pltpu.make_async_copy(
        shapes_ref.at[:, pl.ds(pl.multiple_of(h * OWN, OWN), OWN), :],
        shapes_raw.at[pl.ds(0, MODES)],
        local_sem.at[1],
    )
    shape_copy.start()
    real_copy = pltpu.make_async_copy(real_ref.at[mine], pair.at[0], local_sem.at[2])
    imag_copy = pltpu.make_async_copy(imag_ref.at[mine], pair.at[1], local_sem.at[3])
    real_copy.start()
    imag_copy.start()

    group = [(a, b) for a, b in itertools.product(range(YN), range(2)) if (a, b) != (0, 0)]
    planes = [(a, b) for a, b in itertools.product(range(XN), range(ZN)) if (a, b) != (0, 0)]
    barrier = pltpu.get_barrier_semaphore()

    def greet(device):
        pl.semaphore_signal(barrier, inc=1, device_id=device, device_id_type=MESH)

    def group_device(dy, dh):
        return cell_of(x, z, lax.rem(y + dy, YN)), lax.rem(h + dh, 2)

    def plane_device(dx, dz):
        return cell_of(lax.rem(x + dx, XN), lax.rem(z + dz, ZN), y), h

    edge_cell = jnp.where(h == 0, down_cell, up_cell)
    greet((edge_cell, 0))
    greet((edge_cell, 1))
    for dy, dh in group:
        greet(group_device(dy, dh))
    for dx, dz in planes:
        greet(plane_device(dx, dz))
    pl.semaphore_wait(barrier, 2 + len(group) + len(planes))

    sibling = pltpu.make_async_remote_copy(
        src_ref=source_ref.at[:, :, pl.ds((1 - h) * 29, 35), :],
        dst_ref=stage.at[pl.ds(h * 8, HARM), :, pl.ds(FIRST + 3 * h, 35), :],
        send_sem=send_sem.at[0],
        recv_sem=recv_sem.at[0],
        device_id=(cell, 1 - h),
        device_id_type=MESH,
    )
    high_edge = pltpu.make_async_remote_copy(
        src_ref=source_ref.at[:, pl.ds(0, 3), pl.ds(61, 3), :],
        dst_ref=stage.at[pl.ds(h * 8, HARM), pl.ds(0, 3), pl.ds(FIRST, 3), :],
        send_sem=send_sem.at[1],
        recv_sem=recv_sem.at[1 + h],
        device_id=(up_cell, 0),
        device_id_type=MESH,
    )
    low_edge = pltpu.make_async_remote_copy(
        src_ref=source_ref.at[:, pl.ds(0, 3), pl.ds(0, 3), :],
        dst_ref=stage.at[pl.ds(h * 8, HARM), pl.ds(0, 3), pl.ds(FIRST + 35, 3), :],
        send_sem=send_sem.at[2],
        recv_sem=recv_sem.at[1 + h],
        device_id=(down_cell, 1),
        device_id_type=MESH,
    )
    high_edge.start()
    low_edge.start()
    sibling.start()

    zero = jnp.zeros((ROWS, CHORD), jnp.float32)
    for layer in range(LAYERS):
        stage[7, layer] = zero
        stage[15, layer] = zero
    shapes_wide[pl.ds(MODES * OWN, 4 * OWN), :] = jnp.zeros((4 * OWN, CHORD), jnp.float32)

    shape_copy.wait()

    def widen(m, carry):
        shapes_wide[pl.ds(pl.multiple_of(m * OWN, OWN), OWN), :] = shapes_raw[m].astype(jnp.float32)
        return carry

    lax.fori_loop(0, MODES, widen, 0, unroll=4)

    def flatten(s, carry):
        rows = shapes_wide[pl.ds(s, 64, stride=OWN), :]
        shapes_flat[:, pl.ds(pl.multiple_of(s * CHORD, CHORD), CHORD)] = rows.astype(jnp.bfloat16)
        return carry

    lax.fori_loop(0, OWN, flatten, 0, unroll=4)

    lane = lax.broadcasted_iota(jnp.int32, (64, CHORD), 1)
    left_half = lane < 64
    real_copy.wait()
    imag_copy.wait()
    gauss[...] = jnp.zeros_like(gauss)
    gauss[0:MODES, 0:MODES] = pair[0]
    gauss[64 : 64 + MODES, 0:MODES] = pair[1]
    both = gauss[0:64, :] + pltpu.roll(gauss[64:128, :], 64, 1)
    system = jnp.concatenate([both, jnp.zeros_like(both)], axis=0)
    adjoint = jnp.transpose(system)
    gram = jnp.dot(adjoint, system, precision=HIGHEST, preferred_element_type=jnp.float32)
    top, low = gram[0:64], gram[64:128]
    gauss[0:64, :] = jnp.where(
        left_half, top + pltpu.roll(low, 64, 1), pltpu.roll(adjoint[0:64], 64, 1)
    )
    gauss[64:128, :] = jnp.where(
        left_half, pltpu.roll(top, 64, 1) - low, -pltpu.roll(adjoint[64:128], 64, 1)
    )

    def pivot(k, carry):
        pick = jnp.full((8, CHORD), k, jnp.int32)
        row_re = jnp.broadcast_to(gauss[pl.ds(k, 1), :], (8, CHORD))
        row_im = jnp.broadcast_to(gauss[pl.ds(64 + k, 1), :], (8, CHORD))
        scale = 1.0 / jnp.take_along_axis(row_re, pick, axis=1)
        row_re = row_re * scale
        row_im = row_im * scale
        for block in range(8):
            here, there = pl.ds(8 * block, 8), pl.ds(64 + 8 * block, 8)
            old_re, old_im = gauss[here, :], gauss[there, :]
            col_re = jnp.take_along_axis(old_re, pick, axis=1)
            col_im = jnp.take_along_axis(old_im, pick, axis=1)
            gauss[here, :] = old_re - col_re * row_re + col_im * row_im
            gauss[there, :] = old_im - col_re * row_im - col_im * row_re
        gauss[pl.ds(k, 1), :] = row_re[0:1]
        gauss[pl.ds(64 + k, 1), :] = row_im[0:1]
        return carry

    sub = lax.broadcasted_iota(jnp.int32, (16, CHORD), 0)
    lane16 = lax.broadcasted_iota(jnp.int32, (16, CHORD), 1)
    coupling = jnp.zeros((16, CHORD), jnp.float32)
    for k in range(HARM):
        value = RELAX * freq_ref[k]
        coupling = jnp.where(sub == k, value, jnp.where(sub == 8 + k, -value, coupling))
    not_last = lane16 < CHORD - 1
    not_first = lane16 > 0

    own_copy.wait()
    sibling.wait_recv()
    edge_wait = pltpu.make_async_copy(
        stage.at[pl.ds(0, HARM), pl.ds(0, 3), pl.ds(FIRST, 3), :],
        stage.at[pl.ds(0, HARM), pl.ds(0, 3), pl.ds(FIRST, 3), :],
        recv_sem.at[1],
    )
    edge_wait2 = pltpu.make_async_copy(
        stage.at[pl.ds(0, HARM), pl.ds(0, 3), pl.ds(FIRST, 3), :],
        stage.at[pl.ds(0, HARM), pl.ds(0, 3), pl.ds(FIRST, 3), :],
        recv_sem.at[2],
    )
    edge_wait.wait()
    edge_wait2.wait()

    flat_stage = stage.reshape(16 * LAYERS * ROWS, CHORD)

    def gather(t, carry):
        for layer in range(LAYERS):
            for part in range(2):
                row = part * 8 * LAYERS * ROWS + layer * ROWS + FIRST + t
                first[layer, t, pl.ds(8 * part, 8), :] = flat_stage[
                    pl.ds(row, 8, stride=LAYERS * ROWS), :
                ]
        return carry

    lax.fori_loop(0, SPAN, gather, 0, unroll=2)

    def relaxed(field, layers, layer, t):
        centre = field[layer, t]
        near = field[layer, t + 1] + field[layer, t - 1]
        near = near + jnp.where(not_last, pltpu.roll(centre, CHORD - 1, 1), 0.0)
        near = near + jnp.where(not_first, pltpu.roll(centre, 1, 1), 0.0)
        if layer + 1 < layers:
            near = near + field[layer + 1, t]
        if layer > 0:
            near = near + field[layer - 1, t]
        partner = jnp.concatenate([centre[8:16], centre[0:8]], axis=0)
        return CENTER * centre + coupling * partner + RELAX * (near + first[layer, t])

    def step_one(t, carry):
        for layer in range(3):
            second[layer, t] = relaxed(first, 4, layer, t)
        return carry

    def step_two(t, carry):
        for layer in range(2):
            third[layer, t] = relaxed(second, 3, layer, t)
        return carry

    lax.fori_loop(1, SPAN - 1, step_one, 0, unroll=2)
    lax.fori_loop(2, SPAN - 2, step_two, 0, unroll=2)

    blade_row = h * OWN
    low_blade = blade_ref[blade_row]
    high_blade = blade_ref[blade_row + OWN - 1]
    low_count = jnp.float32(0.0)
    for s in range(OWN):
        value = relaxed(third, 2, 0, s + 3).astype(jnp.bfloat16)
        weight = jnp.where(blade_ref[blade_row + s] == low_blade, jnp.float32(1.0), jnp.float32(0.0))
        low_count = low_count + weight
        wall[:, s * CHORD : (s + 1) * CHORD] = value
        wall_low[:, s * CHORD : (s + 1) * CHORD] = (value.astype(jnp.float32) * weight).astype(
            jnp.bfloat16
        )

    contract = (((1,), (1,)), ((), ()))
    packed[...] = jnp.zeros_like(packed)
    packed[0:16, 0:64] = lax.dot_general(
        wall[...], shapes_flat[...], contract, preferred_element_type=jnp.float32
    )
    packed[16:32, 0:64] = lax.dot_general(
        wall_low[...], shapes_flat[...], contract, preferred_element_type=jnp.float32
    )
    lane8 = lax.broadcasted_iota(jnp.int32, (8, CHORD), 1)
    whole = packed[0:8, :] + pltpu.roll(packed[8:16, :], 64, 1)
    lower = packed[16:24, :] + pltpu.roll(packed[24:32, :], 64, 1)
    upper = whole - lower
    lower = jnp.where(lane8 == 62, low_count, lower)
    upper = jnp.where(lane8 == 62, OWN - low_count, upper)
    low_id = jnp.full((1, CHORD), low_blade, jnp.int32).astype(jnp.float32)
    high_id = jnp.full((1, CHORD), high_blade, jnp.int32).astype(jnp.float32)
    for j in range(8):
        send1[j, 0:1, :] = lower[j : j + 1]
        send1[j, 1:2, :] = upper[j : j + 1]
        send1[j, 2:3, :] = low_id
        send1[j, 3:4, :] = high_id
    recv1[member] = send1[member]
    copies1 = []
    for dy, dh in group:
        to_cell, to_core = group_device(dy, dh)
        copy = pltpu.make_async_remote_copy(
            src_ref=send1.at[lax.rem(y + dy, YN) * 2 + to_core],
            dst_ref=recv1.at[member],
            send_sem=send_sem.at[3],
            recv_sem=recv_sem.at[3],
            device_id=(to_cell, to_core),
            device_id_type=MESH,
        )
        copy.start()
    all1 = pltpu.make_async_copy(recv1.at[pl.ds(0, 7)], recv1.at[pl.ds(0, 7)], recv_sem.at[3])
    lax.fori_loop(0, 20, pivot, 0)
    all1.wait()

    base = recv1[0, 2:3, :]
    sums = [jnp.zeros((1, CHORD), jnp.float32) for _ in range(3)]
    for j in range(8):
        for part in range(2):
            row = recv1[j, part : part + 1, :]
            blade = recv1[j, 2 + part : 3 + part, :] - base
            for r in range(3):
                sums[r] = sums[r] + jnp.where(blade == float(r), row, 0.0)
    for r in range(3):
        send2[r : r + 1, :] = sums[r]
    send2[3:4, :] = base
    recv2[plane] = send2[...]
    for dx, dz in planes:
        copy = pltpu.make_async_remote_copy(
            src_ref=send2,
            dst_ref=recv2.at[plane],
            send_sem=send_sem.at[4],
            recv_sem=recv_sem.at[4],
            device_id=plane_device(dx, dz),
            device_id_type=MESH,
        )
        copy.start()
    all2 = pltpu.make_async_copy(recv2.at[pl.ds(0, 31)], recv2.at[pl.ds(0, 31)], recv_sem.at[4])

    lax.fori_loop(20, MODES, pivot, 0)
    back_re = pltpu.roll(gauss[0:64, :], 64, 1)
    back_im = pltpu.roll(gauss[64:128, :], 64, 1)
    inverse[0:64, :] = jnp.where(left_half, back_re, -gauss[64:128, :])
    inverse[64:128, :] = jnp.where(left_half, back_im, gauss[0:64, :])

    all2.wait()
    everything = recv2[...]
    summed = jnp.sum(everything, axis=0)
    total = summed[0:1] + summed[1:2] + summed[2:3]
    lane1 = lax.broadcasted_iota(jnp.int32, (1, CHORD), 1)
    used = (lane1 < MODES) | ((lane1 >= 64) & (lane1 < 64 + MODES))
    total = jnp.where(used, total * (1.0 / 1024.0), 0.0)
    solved = lax.dot_general(
        jnp.broadcast_to(total, (8, CHORD)), inverse[...], contract,
        precision=HIGHEST, preferred_element_type=jnp.float32,
    )[0:1]
    amplitude = jnp.where(used, solved, 0.0).astype(jnp.bfloat16).astype(jnp.float32)
    row3 = lax.broadcasted_iota(jnp.int32, (32, 4, CHORD), 1).astype(jnp.float32)
    lane3 = lax.broadcasted_iota(jnp.int32, (32, 4, CHORD), 2).astype(jnp.float32)
    belongs = (everything[:, 3:4, :] + row3 == lane3) & (row3 < 3.0)
    dots = jnp.sum(everything * amplitude, axis=2, keepdims=True)
    shares = jnp.sum(jnp.sum(jnp.where(belongs, dots, 0.0), axis=0), axis=0, keepdims=True)

    send3[0:1, :] = amplitude
    send3[1:2, :] = shares
    recv3[member] = send3[...]
    for dy, dh in group:
        copy = pltpu.make_async_remote_copy(
            src_ref=send3,
            dst_ref=recv3.at[member],
            send_sem=send_sem.at[5],
            recv_sem=recv_sem.at[5],
            device_id=group_device(dy, dh),
            device_id_type=MESH,
        )
        copy.start()
    all3 = pltpu.make_async_copy(recv3.at[pl.ds(0, 7)], recv3.at[pl.ds(0, 7)], recv_sem.at[5])

    counted = jnp.sum(jnp.where(lane3 == 62.0, everything, 0.0), axis=2, keepdims=True)
    counts = jnp.sum(jnp.sum(jnp.where(belongs, counted, 0.0), axis=0), axis=0, keepdims=True)
    counts = jnp.where(lane1 < BLADES, counts * CHORD, 1.0)
    all3.wait()

    totals = recv3[0, 1:2, :]
    for j in range(1, 8):
        totals = totals + recv3[j, 1:2, :]
    load_ref[...] = totals * lax.rsqrt(counts)
    amplitudes = jnp.concatenate([recv3[j, 0:1, :] for j in range(8)], axis=0)
    both_parts = jnp.concatenate([amplitudes, pltpu.roll(amplitudes, 64, 1)], axis=0)
    both_parts = both_parts[:, 0:64].astype(jnp.bfloat16)
    for s in range(0, OWN, 4):
        lanes = slice(s * CHORD, (s + 4) * CHORD)
        rebuilt = jnp.dot(both_parts, shapes_flat[:, lanes], preferred_element_type=jnp.float32)
        product = jnp.sum(rebuilt * wall[:, lanes].astype(jnp.float32), axis=0, keepdims=True)
        for i in range(4):
            sens_ref[s + i : s + i + 1, :] = product[:, i * CHORD : (i + 1) * CHORD]

    sibling.wait_send()
    high_edge.wait_send()
    low_edge.wait_send()
    pltpu.make_async_copy(recv1.at[pl.ds(0, 7)], recv1.at[pl.ds(0, 7)], send_sem.at[3]).wait()
    pltpu.make_async_copy(recv2.at[pl.ds(0, 31)], recv2.at[pl.ds(0, 31)], send_sem.at[4]).wait()
    pltpu.make_async_copy(recv3.at[pl.ds(0, 7)], recv3.at[pl.ds(0, 7)], send_sem.at[5]).wait()


def per_device(source, mode_shapes, modal_real, modal_imag, harmonic_freq, blade_of_row):
    f32, bf16 = jnp.float32, jnp.bfloat16
    any_space = pl.BlockSpec(memory_space=pl.ANY)
    smem = pl.BlockSpec(memory_space=pltpu.SMEM)
    vmem = pl.BlockSpec(memory_space=pltpu.VMEM)
    sens, load = pl.pallas_call(
        kernel,
        name="flutter",
        out_shape=(
            jax.ShapeDtypeStruct((OWN, CHORD), f32),
            jax.ShapeDtypeStruct((1, CHORD), f32),
        ),
        in_specs=[smem, smem, any_space, any_space, any_space, any_space],
        out_specs=(vmem, vmem),
        scratch_shapes=[
            pltpu.VMEM((16, LAYERS, ROWS, CHORD), f32),
            pltpu.VMEM((MODES, OWN, CHORD), bf16),
            pltpu.VMEM((64 * OWN, CHORD), f32),
            pltpu.VMEM((64, OWN * CHORD), bf16),
            pltpu.VMEM((LAYERS, SPAN, 16, CHORD), f32),
            pltpu.VMEM((3, SPAN, 16, CHORD), f32),
            pltpu.VMEM((2, SPAN, 16, CHORD), f32),
            pltpu.VMEM((16, OWN * CHORD), bf16),
            pltpu.VMEM((16, OWN * CHORD), bf16),
            pltpu.VMEM((2, MODES, MODES), f32),
            pltpu.VMEM((CHORD, CHORD), f32),
            pltpu.VMEM((CHORD, CHORD), f32),
            pltpu.VMEM((32, CHORD), f32),
            pltpu.VMEM((8, 4, CHORD), f32),
            pltpu.VMEM((8, 4, CHORD), f32),
            pltpu.VMEM((4, CHORD), f32),
            pltpu.VMEM((32, 4, CHORD), f32),
            pltpu.VMEM((2, CHORD), f32),
            pltpu.VMEM((8, 2, CHORD), f32),
            pltpu.SemaphoreType.DMA((4,)),
            pltpu.SemaphoreType.DMA((6,)),
            pltpu.SemaphoreType.DMA((6,)),
        ],
        compiler_params=pltpu.CompilerParams(
            collective_id=0, has_side_effects=True, vmem_limit_bytes=24 * 1024 * 1024
        ),
    )(harmonic_freq, blade_of_row, source, mode_shapes, modal_real, modal_imag)
    return sens, load[0, :BLADES]


def solution(mesh):
    placed = (P("harm", None, "cells", None), P(None, "cells", None), P(), P(), P(), P("cells"))
    return jax.shard_map(
        per_device,
        mesh=mesh,
        in_specs=placed,
        out_specs=(P(("cells", "harm"), None), P()),
        check_vma=False,
    )
```

```python
import itertools

import jax
import jax.numpy as jnp
from jax import lax
from jax.experimental import pallas as pl
from jax.experimental.pallas import tpu as pltpu
from jax.sharding import PartitionSpec as P

BLADES = 24
RELAX = 0.15
DAMPING = 0.5
CENTER = 1.0 - 6.0 * RELAX - RELAX * DAMPING

HARM = 7
MODES = 60
LAYERS = 4
CHORD = 128
OWN = 32
ROWS = 48
FIRST = 5
SPAN = 38
XN, ZN, YN = 4, 8, 4
MESH = pl.DeviceIdType.MESH
HIGHEST = lax.Precision.HIGHEST


def place():
    cell = lax.axis_index("cells")
    return cell // (ZN * YN), (cell // YN) % ZN, cell % YN, lax.axis_index("harm")


def cell_of(x, z, y):
    return (x * ZN + z) * YN + y


def kernel(
    freq_hbm, blade_hbm, source_ref, shapes_ref, real_ref, imag_ref,
    sens_ref, load_ref,
    stage, shapes_raw, shapes_wide, shapes_flat, first, second, third, wall, wall_low,
    pair, gauss, inverse, packed, send1, recv1, send2, recv2, send3, recv3,
    freq_ref, blade_ref, local_sem, send_sem, recv_sem,
):
    x, z, y, h = place()
    cell = lax.axis_index("cells")
    cells = XN * ZN * YN
    member = y * 2 + h
    plane = x * ZN + z
    up_cell = lax.rem(cell + 1, cells)
    down_cell = lax.rem(cell + cells - 1, cells)
    mine = jnp.minimum(member, HARM - 1)

    start = h * 29
    own_row = 8 - 3 * h
    own_copy = pltpu.make_async_copy(
        source_ref.at[:, :, pl.ds(start, 35), :],
        stage.at[pl.ds(h * 8, HARM), :, pl.ds(own_row, 35), :],
        local_sem.at[0],
    )
    own_copy.start()
    shape_copy = pltpu.make_async_copy(
        shapes_ref.at[:, pl.ds(pl.multiple_of(h * OWN, OWN), OWN), :],
        shapes_raw.at[pl.ds(0, MODES)],
        local_sem.at[1],
    )
    shape_copy.start()
    real_copy = pltpu.make_async_copy(real_ref.at[mine], pair.at[0], local_sem.at[2])
    imag_copy = pltpu.make_async_copy(imag_ref.at[mine], pair.at[1], local_sem.at[3])
    freq_copy = pltpu.make_async_copy(freq_hbm, freq_ref, local_sem.at[4])
    blade_copy = pltpu.make_async_copy(blade_hbm, blade_ref, local_sem.at[5])
    real_copy.start()
    imag_copy.start()
    freq_copy.start()
    blade_copy.start()

    group = [(a, b) for a, b in itertools.product(range(YN), range(2)) if (a, b) != (0, 0)]
    planes = [(a, b) for a, b in itertools.product(range(XN), range(ZN)) if (a, b) != (0, 0)]
    barrier = pltpu.get_barrier_semaphore()

    def greet(device):
        pl.semaphore_signal(barrier, inc=1, device_id=device, device_id_type=MESH)

    def group_device(dy, dh):
        return cell_of(x, z, lax.rem(y + dy, YN)), lax.rem(h + dh, 2)

    def plane_device(dx, dz):
        return cell_of(lax.rem(x + dx, XN), lax.rem(z + dz, ZN), y), h

    edge_cell = jnp.where(h == 0, down_cell, up_cell)
    greet((edge_cell, 0))
    greet((edge_cell, 1))
    for dy, dh in group:
        greet(group_device(dy, dh))
    for dx, dz in planes:
        greet(plane_device(dx, dz))
    pl.semaphore_wait(barrier, 2 + len(group) + len(planes))

    sibling = pltpu.make_async_remote_copy(
        src_ref=source_ref.at[:, :, pl.ds((1 - h) * 29, 35), :],
        dst_ref=stage.at[pl.ds(h * 8, HARM), :, pl.ds(FIRST + 3 * h, 35), :],
        send_sem=send_sem.at[0],
        recv_sem=recv_sem.at[0],
        device_id=(cell, 1 - h),
        device_id_type=MESH,
    )
    high_edge = pltpu.make_async_remote_copy(
        src_ref=source_ref.at[:, pl.ds(0, 3), pl.ds(61, 3), :],
        dst_ref=stage.at[pl.ds(h * 8, HARM), pl.ds(0, 3), pl.ds(FIRST, 3), :],
        send_sem=send_sem.at[1],
        recv_sem=recv_sem.at[1 + h],
        device_id=(up_cell, 0),
        device_id_type=MESH,
    )
    low_edge = pltpu.make_async_remote_copy(
        src_ref=source_ref.at[:, pl.ds(0, 3), pl.ds(0, 3), :],
        dst_ref=stage.at[pl.ds(h * 8, HARM), pl.ds(0, 3), pl.ds(FIRST + 35, 3), :],
        send_sem=send_sem.at[2],
        recv_sem=recv_sem.at[1 + h],
        device_id=(down_cell, 1),
        device_id_type=MESH,
    )
    high_edge.start()
    low_edge.start()
    sibling.start()

    zero = jnp.zeros((ROWS, CHORD), jnp.float32)
    for layer in range(LAYERS):
        stage[7, layer] = zero
        stage[15, layer] = zero
    shapes_wide[pl.ds(MODES * OWN, 4 * OWN), :] = jnp.zeros((4 * OWN, CHORD), jnp.float32)

    shape_copy.wait()

    def widen(m, carry):
        shapes_wide[pl.ds(pl.multiple_of(m * OWN, OWN), OWN), :] = shapes_raw[m].astype(jnp.float32)
        return carry

    lax.fori_loop(0, MODES, widen, 0, unroll=4)

    def flatten(s, carry):
        rows = shapes_wide[pl.ds(s, 64, stride=OWN), :]
        shapes_flat[:, pl.ds(pl.multiple_of(s * CHORD, CHORD), CHORD)] = rows.astype(jnp.bfloat16)
        return carry

    lax.fori_loop(0, OWN, flatten, 0, unroll=4)

    lane = lax.broadcasted_iota(jnp.int32, (64, CHORD), 1)
    left_half = lane < 64
    real_copy.wait()
    imag_copy.wait()
    gauss[...] = jnp.zeros_like(gauss)
    gauss[0:MODES, 0:MODES] = pair[0]
    gauss[64 : 64 + MODES, 0:MODES] = pair[1]
    both = gauss[0:64, :] + pltpu.roll(gauss[64:128, :], 64, 1)
    system = jnp.concatenate([both, jnp.zeros_like(both)], axis=0)
    adjoint = jnp.transpose(system)
    gram = jnp.dot(adjoint, system, precision=HIGHEST, preferred_element_type=jnp.float32)
    top, low = gram[0:64], gram[64:128]
    gauss[0:64, :] = jnp.where(
        left_half, top + pltpu.roll(low, 64, 1), pltpu.roll(adjoint[0:64], 64, 1)
    )
    gauss[64:128, :] = jnp.where(
        left_half, pltpu.roll(top, 64, 1) - low, -pltpu.roll(adjoint[64:128], 64, 1)
    )

    def pivot(k, carry):
        pick = jnp.full((8, CHORD), k, jnp.int32)
        row_re = jnp.broadcast_to(gauss[pl.ds(k, 1), :], (8, CHORD))
        row_im = jnp.broadcast_to(gauss[pl.ds(64 + k, 1), :], (8, CHORD))
        scale = 1.0 / jnp.take_along_axis(row_re, pick, axis=1)
        row_re = row_re * scale
        row_im = row_im * scale
        for block in range(8):
            here, there = pl.ds(8 * block, 8), pl.ds(64 + 8 * block, 8)
            old_re, old_im = gauss[here, :], gauss[there, :]
            col_re = jnp.take_along_axis(old_re, pick, axis=1)
            col_im = jnp.take_along_axis(old_im, pick, axis=1)
            gauss[here, :] = old_re - col_re * row_re + col_im * row_im
            gauss[there, :] = old_im - col_re * row_im - col_im * row_re
        gauss[pl.ds(k, 1), :] = row_re[0:1]
        gauss[pl.ds(64 + k, 1), :] = row_im[0:1]
        return carry

    sub = lax.broadcasted_iota(jnp.int32, (16, CHORD), 0)
    lane16 = lax.broadcasted_iota(jnp.int32, (16, CHORD), 1)
    freq_copy.wait()
    blade_copy.wait()
    coupling = jnp.zeros((16, CHORD), jnp.float32)
    for k in range(HARM):
        value = RELAX * freq_ref[k]
        coupling = jnp.where(sub == k, value, jnp.where(sub == 8 + k, -value, coupling))
    not_last = lane16 < CHORD - 1
    not_first = lane16 > 0

    own_copy.wait()
    sibling.wait_recv()
    edge_wait = pltpu.make_async_copy(
        stage.at[pl.ds(0, HARM), pl.ds(0, 3), pl.ds(FIRST, 3), :],
        stage.at[pl.ds(0, HARM), pl.ds(0, 3), pl.ds(FIRST, 3), :],
        recv_sem.at[1],
    )
    edge_wait2 = pltpu.make_async_copy(
        stage.at[pl.ds(0, HARM), pl.ds(0, 3), pl.ds(FIRST, 3), :],
        stage.at[pl.ds(0, HARM), pl.ds(0, 3), pl.ds(FIRST, 3), :],
        recv_sem.at[2],
    )
    edge_wait.wait()
    edge_wait2.wait()

    flat_stage = stage.reshape(16 * LAYERS * ROWS, CHORD)

    def gather(t, carry):
        for layer in range(LAYERS):
            for part in range(2):
                row = part * 8 * LAYERS * ROWS + layer * ROWS + FIRST + t
                first[layer, t, pl.ds(8 * part, 8), :] = flat_stage[
                    pl.ds(row, 8, stride=LAYERS * ROWS), :
                ]
        return carry

    lax.fori_loop(0, SPAN, gather, 0, unroll=2)

    def relaxed(field, layers, layer, t):
        centre = field[layer, t]
        near = field[layer, t + 1] + field[layer, t - 1]
        near = near + jnp.where(not_last, pltpu.roll(centre, CHORD - 1, 1), 0.0)
        near = near + jnp.where(not_first, pltpu.roll(centre, 1, 1), 0.0)
        if layer + 1 < layers:
            near = near + field[layer + 1, t]
        if layer > 0:
            near = near + field[layer - 1, t]
        partner = jnp.concatenate([centre[8:16], centre[0:8]], axis=0)
        return CENTER * centre + coupling * partner + RELAX * (near + first[layer, t])

    def step_one(t, carry):
        for layer in range(3):
            second[layer, t] = relaxed(first, 4, layer, t)
        return carry

    def step_two(t, carry):
        for layer in range(2):
            third[layer, t] = relaxed(second, 3, layer, t)
        return carry

    lax.fori_loop(1, SPAN - 1, step_one, 0, unroll=2)
    lax.fori_loop(2, SPAN - 2, step_two, 0, unroll=2)

    blade_row = h * OWN
    low_blade = blade_ref[blade_row]
    high_blade = blade_ref[blade_row + OWN - 1]
    low_count = jnp.float32(0.0)
    for s in range(OWN):
        value = relaxed(third, 2, 0, s + 3).astype(jnp.bfloat16)
        weight = jnp.where(blade_ref[blade_row + s] == low_blade, jnp.float32(1.0), jnp.float32(0.0))
        low_count = low_count + weight
        wall[:, s * CHORD : (s + 1) * CHORD] = value
        wall_low[:, s * CHORD : (s + 1) * CHORD] = (value.astype(jnp.float32) * weight).astype(
            jnp.bfloat16
        )

    contract = (((1,), (1,)), ((), ()))
    packed[...] = jnp.zeros_like(packed)
    packed[0:16, 0:64] = lax.dot_general(
        wall[...], shapes_flat[...], contract, preferred_element_type=jnp.float32
    )
    packed[16:32, 0:64] = lax.dot_general(
        wall_low[...], shapes_flat[...], contract, preferred_element_type=jnp.float32
    )
    lane8 = lax.broadcasted_iota(jnp.int32, (8, CHORD), 1)
    whole = packed[0:8, :] + pltpu.roll(packed[8:16, :], 64, 1)
    lower = packed[16:24, :] + pltpu.roll(packed[24:32, :], 64, 1)
    upper = whole - lower
    lower = jnp.where(lane8 == 62, low_count, lower)
    upper = jnp.where(lane8 == 62, OWN - low_count, upper)
    low_id = jnp.full((1, CHORD), low_blade, jnp.int32).astype(jnp.float32)
    high_id = jnp.full((1, CHORD), high_blade, jnp.int32).astype(jnp.float32)
    for j in range(8):
        send1[j, 0:1, :] = lower[j : j + 1]
        send1[j, 1:2, :] = upper[j : j + 1]
        send1[j, 2:3, :] = low_id
        send1[j, 3:4, :] = high_id
    recv1[member] = send1[member]
    copies1 = []
    for dy, dh in group:
        to_cell, to_core = group_device(dy, dh)
        copy = pltpu.make_async_remote_copy(
            src_ref=send1.at[lax.rem(y + dy, YN) * 2 + to_core],
            dst_ref=recv1.at[member],
            send_sem=send_sem.at[3],
            recv_sem=recv_sem.at[3],
            device_id=(to_cell, to_core),
            device_id_type=MESH,
        )
        copy.start()
    all1 = pltpu.make_async_copy(recv1.at[pl.ds(0, 7)], recv1.at[pl.ds(0, 7)], recv_sem.at[3])
    lax.fori_loop(0, 20, pivot, 0)
    all1.wait()

    base = recv1[0, 2:3, :]
    sums = [jnp.zeros((1, CHORD), jnp.float32) for _ in range(3)]
    for j in range(8):
        for part in range(2):
            row = recv1[j, part : part + 1, :]
            blade = recv1[j, 2 + part : 3 + part, :] - base
            for r in range(3):
                sums[r] = sums[r] + jnp.where(blade == float(r), row, 0.0)
    for r in range(3):
        send2[r : r + 1, :] = sums[r]
    send2[3:4, :] = base
    recv2[plane] = send2[...]
    for dx, dz in planes:
        copy = pltpu.make_async_remote_copy(
            src_ref=send2,
            dst_ref=recv2.at[plane],
            send_sem=send_sem.at[4],
            recv_sem=recv_sem.at[4],
            device_id=plane_device(dx, dz),
            device_id_type=MESH,
        )
        copy.start()
    all2 = pltpu.make_async_copy(recv2.at[pl.ds(0, 31)], recv2.at[pl.ds(0, 31)], recv_sem.at[4])

    lax.fori_loop(20, MODES, pivot, 0)
    back_re = pltpu.roll(gauss[0:64, :], 64, 1)
    back_im = pltpu.roll(gauss[64:128, :], 64, 1)
    inverse[0:64, :] = jnp.where(left_half, back_re, -gauss[64:128, :])
    inverse[64:128, :] = jnp.where(left_half, back_im, gauss[0:64, :])

    all2.wait()
    everything = recv2[...]
    summed = jnp.sum(everything, axis=0)
    total = summed[0:1] + summed[1:2] + summed[2:3]
    lane1 = lax.broadcasted_iota(jnp.int32, (1, CHORD), 1)
    used = (lane1 < MODES) | ((lane1 >= 64) & (lane1 < 64 + MODES))
    total = jnp.where(used, total * (1.0 / 1024.0), 0.0)
    solved = lax.dot_general(
        jnp.broadcast_to(total, (8, CHORD)), inverse[...], contract,
        precision=HIGHEST, preferred_element_type=jnp.float32,
    )[0:1]
    amplitude = jnp.where(used, solved, 0.0).astype(jnp.bfloat16).astype(jnp.float32)
    row3 = lax.broadcasted_iota(jnp.int32, (32, 4, CHORD), 1).astype(jnp.float32)
    lane3 = lax.broadcasted_iota(jnp.int32, (32, 4, CHORD), 2).astype(jnp.float32)
    belongs = (everything[:, 3:4, :] + row3 == lane3) & (row3 < 3.0)
    dots = jnp.sum(everything * amplitude, axis=2, keepdims=True)
    shares = jnp.sum(jnp.sum(jnp.where(belongs, dots, 0.0), axis=0), axis=0, keepdims=True)

    send3[0:1, :] = amplitude
    send3[1:2, :] = shares
    recv3[member] = send3[...]
    for dy, dh in group:
        copy = pltpu.make_async_remote_copy(
            src_ref=send3,
            dst_ref=recv3.at[member],
            send_sem=send_sem.at[5],
            recv_sem=recv_sem.at[5],
            device_id=group_device(dy, dh),
            device_id_type=MESH,
        )
        copy.start()
    all3 = pltpu.make_async_copy(recv3.at[pl.ds(0, 7)], recv3.at[pl.ds(0, 7)], recv_sem.at[5])

    counted = jnp.sum(jnp.where(lane3 == 62.0, everything, 0.0), axis=2, keepdims=True)
    counts = jnp.sum(jnp.sum(jnp.where(belongs, counted, 0.0), axis=0), axis=0, keepdims=True)
    counts = jnp.where(lane1 < BLADES, counts * CHORD, 1.0)
    all3.wait()

    totals = recv3[0, 1:2, :]
    for j in range(1, 8):
        totals = totals + recv3[j, 1:2, :]
    load_ref[...] = totals * lax.rsqrt(counts)
    amplitudes = jnp.concatenate([recv3[j, 0:1, :] for j in range(8)], axis=0)
    both_parts = jnp.concatenate([amplitudes, pltpu.roll(amplitudes, 64, 1)], axis=0)
    both_parts = both_parts[:, 0:64].astype(jnp.bfloat16)
    for s in range(0, OWN, 4):
        lanes = slice(s * CHORD, (s + 4) * CHORD)
        rebuilt = jnp.dot(both_parts, shapes_flat[:, lanes], preferred_element_type=jnp.float32)
        product = jnp.sum(rebuilt * wall[:, lanes].astype(jnp.float32), axis=0, keepdims=True)
        for i in range(4):
            sens_ref[s + i : s + i + 1, :] = product[:, i * CHORD : (i + 1) * CHORD]

    sibling.wait_send()
    high_edge.wait_send()
    low_edge.wait_send()
    pltpu.make_async_copy(recv1.at[pl.ds(0, 7)], recv1.at[pl.ds(0, 7)], send_sem.at[3]).wait()
    pltpu.make_async_copy(recv2.at[pl.ds(0, 31)], recv2.at[pl.ds(0, 31)], send_sem.at[4]).wait()
    pltpu.make_async_copy(recv3.at[pl.ds(0, 7)], recv3.at[pl.ds(0, 7)], send_sem.at[5]).wait()


def per_device(source, mode_shapes, modal_real, modal_imag, harmonic_freq, blade_of_row):
    f32, bf16 = jnp.float32, jnp.bfloat16
    operands = (harmonic_freq, blade_of_row, source, mode_shapes, modal_real, modal_imag)
    hbm = pl.BlockSpec(memory_space=pltpu.HBM)
    vmem = pl.BlockSpec(memory_space=pltpu.VMEM)
    sens, load = pl.pallas_call(
        kernel,
        name="flutter",
        out_shape=(
            pltpu.VMEM((OWN, CHORD), f32),
            pltpu.VMEM((1, CHORD), f32),
        ),
        in_specs=[hbm] * 6,
        out_specs=(vmem, vmem),
        scratch_shapes=[
            pltpu.VMEM((16, LAYERS, ROWS, CHORD), f32),
            pltpu.VMEM((MODES, OWN, CHORD), bf16),
            pltpu.VMEM((64 * OWN, CHORD), f32),
            pltpu.VMEM((64, OWN * CHORD), bf16),
            pltpu.VMEM((LAYERS, SPAN, 16, CHORD), f32),
            pltpu.VMEM((3, SPAN, 16, CHORD), f32),
            pltpu.VMEM((2, SPAN, 16, CHORD), f32),
            pltpu.VMEM((16, OWN * CHORD), bf16),
            pltpu.VMEM((16, OWN * CHORD), bf16),
            pltpu.VMEM((2, MODES, MODES), f32),
            pltpu.VMEM((CHORD, CHORD), f32),
            pltpu.VMEM((CHORD, CHORD), f32),
            pltpu.VMEM((32, CHORD), f32),
            pltpu.VMEM((8, 4, CHORD), f32),
            pltpu.VMEM((8, 4, CHORD), f32),
            pltpu.VMEM((4, CHORD), f32),
            pltpu.VMEM((32, 4, CHORD), f32),
            pltpu.VMEM((2, CHORD), f32),
            pltpu.VMEM((8, 2, CHORD), f32),
            pltpu.SMEM((HARM,), f32),
            pltpu.SMEM((2 * OWN,), jnp.int32),
            pltpu.SemaphoreType.DMA((6,)),
            pltpu.SemaphoreType.DMA((6,)),
            pltpu.SemaphoreType.DMA((6,)),
        ],
        compiler_params=pltpu.CompilerParams(
            collective_id=0, has_side_effects=True, vmem_limit_bytes=32 * 1024 * 1024
        ),
    )(*(pltpu.with_memory_space_constraint(a, pltpu.HBM) for a in operands))
    return sens, load[0, :BLADES]


def solution(mesh):
    placed = (P("harm", None, "cells", None), P(None, "cells", None), P(), P(), P(), P("cells"))
    return jax.shard_map(
        per_device,
        mesh=mesh,
        in_specs=placed,
        out_specs=(P(("cells", "harm"), None), P()),
        check_vma=False,
    )
```

```python
import itertools

import jax
import jax.numpy as jnp
from jax import lax
from jax.experimental import pallas as pl
from jax.experimental.pallas import tpu as pltpu
from jax.sharding import PartitionSpec as P

BLADES = 24
RELAX = 0.15
DAMPING = 0.5
CENTER = 1.0 - 6.0 * RELAX - RELAX * DAMPING

HARM = 7
MODES = 60
LAYERS = 4
CHORD = 128
OWN = 32
SPAN = 38
XN, ZN, YN = 4, 8, 4
MESH = pl.DeviceIdType.MESH
HIGHEST = lax.Precision.HIGHEST


def place():
    cell = lax.axis_index("cells")
    return cell // (ZN * YN), (cell // YN) % ZN, cell % YN, lax.axis_index("harm")


def cell_of(x, z, y):
    return (x * ZN + z) * YN + y


def kernel(
    freq_hbm, blade_hbm, source_ref, shapes_ref, real_ref, imag_ref,
    sens_ref, load_ref,
    shapes_raw, shapes_wide, shapes_flat, first, second, third, wall, wall_low,
    pair, gauss, inverse, packed, send1, recv1, send2, recv2, send3, recv3,
    freq_ref, blade_ref, local_sem, send_sem, recv_sem, known_sem,
):
    x, z, y, h = place()
    cell = lax.axis_index("cells")
    cells = XN * ZN * YN
    member = y * 2 + h
    plane = x * ZN + z
    up_cell = lax.rem(cell + 1, cells)
    down_cell = lax.rem(cell + cells - 1, cells)
    mine = jnp.minimum(member, HARM - 1)

    group = [(a, b) for a, b in itertools.product(range(YN), range(2)) if (a, b) != (0, 0)]
    planes = [(a, b) for a, b in itertools.product(range(XN), range(ZN)) if (a, b) != (0, 0)]
    barrier = pltpu.get_barrier_semaphore()

    def group_device(dy, dh):
        return cell_of(x, z, lax.rem(y + dy, YN)), lax.rem(h + dh, 2)

    def plane_device(dx, dz):
        return cell_of(lax.rem(x + dx, XN), lax.rem(z + dz, ZN), y), h

    edge_cell = jnp.where(h == 0, down_cell, up_cell)
    nearby = [(edge_cell, 0), (edge_cell, 1)]
    nearby += [group_device(dy, dh) for dy, dh in group]
    nearby += [plane_device(dx, 0) for dx in range(1, XN)]
    nearby += [plane_device(0, dz) for dz in (1, 2, ZN - 2, ZN - 1)]
    for device in nearby:
        pl.semaphore_signal(barrier, inc=1, device_id=device, device_id_type=MESH)

    start = h * 29
    for c in range(HARM):
        pltpu.make_async_copy(
            source_ref.at[c, :, pl.ds(start, 35), :],
            first.at[:, pl.ds(3 - 3 * h, 35), h * 8 + c, :],
            local_sem.at[0],
        ).start()
    shape_copy = pltpu.make_async_copy(
        shapes_ref.at[:, pl.ds(pl.multiple_of(h * OWN, OWN), OWN), :],
        shapes_raw.at[pl.ds(0, MODES)],
        local_sem.at[1],
    )
    shape_copy.start()
    real_copy = pltpu.make_async_copy(real_ref.at[mine], pair.at[0], local_sem.at[2])
    imag_copy = pltpu.make_async_copy(imag_ref.at[mine], pair.at[1], local_sem.at[3])
    freq_copy = pltpu.make_async_copy(freq_hbm, freq_ref, local_sem.at[4])
    blade_copy = pltpu.make_async_copy(blade_hbm, blade_ref, local_sem.at[5])
    real_copy.start()
    imag_copy.start()
    freq_copy.start()
    blade_copy.start()
    pl.semaphore_wait(barrier, len(nearby))

    for c in range(HARM):
        pltpu.make_async_remote_copy(
            src_ref=source_ref.at[c, pl.ds(0, 3), pl.ds(61, 3), :],
            dst_ref=first.at[pl.ds(0, 3), pl.ds(0, 3), h * 8 + c, :],
            send_sem=send_sem.at[1],
            recv_sem=recv_sem.at[1],
            device_id=(up_cell, 0),
            device_id_type=MESH,
        ).start()
        pltpu.make_async_remote_copy(
            src_ref=source_ref.at[c, pl.ds(0, 3), pl.ds(0, 3), :],
            dst_ref=first.at[pl.ds(0, 3), pl.ds(35, 3), h * 8 + c, :],
            send_sem=send_sem.at[2],
            recv_sem=recv_sem.at[1],
            device_id=(down_cell, 1),
            device_id_type=MESH,
        ).start()
    for c in range(HARM):
        pltpu.make_async_remote_copy(
            src_ref=source_ref.at[c, :, pl.ds((1 - h) * 29, 35), :],
            dst_ref=first.at[:, pl.ds(3 * h, 35), h * 8 + c, :],
            send_sem=send_sem.at[0],
            recv_sem=recv_sem.at[0],
            device_id=(cell, 1 - h),
            device_id_type=MESH,
        ).start()

    def arrived(array, sem):
        pltpu.make_async_copy(array, array, sem).wait()

    for dz in (2, ZN - 2):
        pl.semaphore_signal(
            known_sem.at[0], inc=1, device_id=plane_device(0, dz), device_id_type=MESH
        )

    shapes_wide[pl.ds(MODES * OWN, 4 * OWN), :] = jnp.zeros((4 * OWN, CHORD), jnp.float32)

    shape_copy.wait()

    def widen(m, carry):
        shapes_wide[pl.ds(pl.multiple_of(m * OWN, OWN), OWN), :] = shapes_raw[m].astype(jnp.float32)
        return carry

    lax.fori_loop(0, MODES, widen, 0, unroll=4)

    def flatten(s, carry):
        rows = shapes_wide[pl.ds(s, 64, stride=OWN), :]
        shapes_flat[:, pl.ds(pl.multiple_of(s * CHORD, CHORD), CHORD)] = rows.astype(jnp.bfloat16)
        return carry

    lax.fori_loop(0, OWN, flatten, 0, unroll=4)

    pl.semaphore_wait(known_sem.at[0], 2)
    for dx in range(1, XN):
        pl.semaphore_signal(
            known_sem.at[1], inc=1, device_id=plane_device(dx, 0), device_id_type=MESH
        )

    sub = lax.broadcasted_iota(jnp.int32, (16, CHORD), 0)
    lane16 = lax.broadcasted_iota(jnp.int32, (16, CHORD), 1)
    freq_copy.wait()
    blade_copy.wait()
    coupling = jnp.zeros((16, CHORD), jnp.float32)
    for k in range(HARM):
        value = RELAX * freq_ref[k]
        coupling = jnp.where(sub == k, value, jnp.where(sub == 8 + k, -value, coupling))
    not_last = lane16 < CHORD - 1
    not_first = lane16 > 0

    def relaxed(field, layers, layer, t):
        centre = field[layer, t]
        near = field[layer, t + 1] + field[layer, t - 1]
        near = near + jnp.where(not_last, pltpu.roll(centre, CHORD - 1, 1), 0.0)
        near = near + jnp.where(not_first, pltpu.roll(centre, 1, 1), 0.0)
        if layer + 1 < layers:
            near = near + field[layer + 1, t]
        if layer > 0:
            near = near + field[layer - 1, t]
        partner = jnp.concatenate([centre[8:16], centre[0:8]], axis=0)
        return CENTER * centre + coupling * partner + RELAX * (near + first[layer, t])

    blade_row = h * OWN
    low_blade = blade_ref[blade_row]
    high_blade = blade_ref[blade_row + OWN - 1]
    low_count = jnp.float32(0.0)
    for s in range(OWN):
        same = blade_ref[blade_row + s] == low_blade
        low_count = low_count + jnp.where(same, jnp.float32(1.0), jnp.float32(0.0))
    in_use = (sub != 7) & (sub != 15)

    def relax_rows(first_t, second_t, third_t, first_n, second_n, third_n):
        def step_one(i, carry):
            for layer in range(3):
                second[layer, first_t + i] = relaxed(first, 4, layer, first_t + i)
            return carry

        def step_two(i, carry):
            for layer in range(2):
                third[layer, second_t + i] = relaxed(second, 3, layer, second_t + i)
            return carry

        def step_three(i, carry):
            s = third_t - 3 + i
            value = jnp.where(in_use, relaxed(third, 2, 0, third_t + i), 0.0).astype(jnp.bfloat16)
            same = blade_ref[blade_row + s] == low_blade
            weight = jnp.where(same, jnp.float32(1.0), jnp.float32(0.0))
            lanes = pl.ds(pl.multiple_of(s * CHORD, CHORD), CHORD)
            wall[:, lanes] = value
            wall_low[:, lanes] = (value.astype(jnp.float32) * weight).astype(jnp.bfloat16)
            return carry

        lax.fori_loop(0, first_n, step_one, 0, unroll=min(first_n, 11))
        lax.fori_loop(0, second_n, step_two, 0, unroll=min(second_n, 16))
        lax.fori_loop(0, third_n, step_three, 0, unroll=True)

    contract = (((1,), (1,)), ((), ()))

    def loads(lanes):
        shapes = shapes_flat[:, lanes]
        for row, part in ((0, wall), (16, wall_low)):
            packed[row : row + 16, 0:64] += lax.dot_general(
                part[:, lanes], shapes, contract, preferred_element_type=jnp.float32
            )

    edge_lanes = pl.ds(pl.multiple_of(h * (29 * CHORD), CHORD), 3 * CHORD)
    wall[:, edge_lanes] = jnp.zeros((16, 3 * CHORD), jnp.bfloat16)
    wall_low[:, edge_lanes] = jnp.zeros((16, 3 * CHORD), jnp.bfloat16)
    packed[...] = jnp.zeros_like(packed)
    halves = first.at[:, pl.ds(0, 35), pl.ds(0, HARM), :]
    arrived(halves, local_sem.at[0])
    arrived(halves, recv_sem.at[0])
    relax_rows(4 - 3 * h, 4 - 2 * h, 6 - 3 * h, 33, 32, 29)
    loads(pl.ds(0, OWN * CHORD))
    edges = first.at[pl.ds(0, 3), pl.ds(0, 6), pl.ds(0, HARM), :]
    arrived(edges, recv_sem.at[1])
    relax_rows(1 + 33 * h, 2 + 31 * h, 3 + 29 * h, 3, 3, 3)
    loads(edge_lanes)

    lane8 = lax.broadcasted_iota(jnp.int32, (8, CHORD), 1)
    whole = packed[0:8, :] + pltpu.roll(packed[8:16, :], 64, 1)
    lower = packed[16:24, :] + pltpu.roll(packed[24:32, :], 64, 1)
    upper = whole - lower
    lower = jnp.where(lane8 == 62, low_count, lower)
    upper = jnp.where(lane8 == 62, OWN - low_count, upper)
    low_id = jnp.full((1, CHORD), low_blade, jnp.int32).astype(jnp.float32)
    high_id = jnp.full((1, CHORD), high_blade, jnp.int32).astype(jnp.float32)
    for j in range(8):
        send1[j, 0:1, :] = lower[j : j + 1]
        send1[j, 1:2, :] = upper[j : j + 1]
        send1[j, 2:3, :] = low_id
        send1[j, 3:4, :] = high_id
    recv1[member] = send1[member]
    for dy, dh in group:
        to_cell, to_core = group_device(dy, dh)
        copy = pltpu.make_async_remote_copy(
            src_ref=send1.at[lax.rem(y + dy, YN) * 2 + to_core],
            dst_ref=recv1.at[member],
            send_sem=send_sem.at[3],
            recv_sem=recv_sem.at[3],
            device_id=(to_cell, to_core),
            device_id_type=MESH,
        )
        copy.start()

    lane = lax.broadcasted_iota(jnp.int32, (64, CHORD), 1)
    left_half = lane < 64
    real_copy.wait()
    imag_copy.wait()
    gauss[...] = jnp.zeros_like(gauss)
    gauss[0:MODES, 0:MODES] = pair[0]
    gauss[64 : 64 + MODES, 0:MODES] = pair[1]
    both = gauss[0:64, :] + pltpu.roll(gauss[64:128, :], 64, 1)
    system = jnp.concatenate([both, jnp.zeros_like(both)], axis=0)
    adjoint = jnp.transpose(system)
    gram = jnp.dot(adjoint, system, precision=HIGHEST, preferred_element_type=jnp.float32)
    top, low = gram[0:64], gram[64:128]
    gauss[0:64, :] = jnp.where(
        left_half, top + pltpu.roll(low, 64, 1), pltpu.roll(adjoint[0:64], 64, 1)
    )
    gauss[64:128, :] = jnp.where(
        left_half, pltpu.roll(top, 64, 1) - low, -pltpu.roll(adjoint[64:128], 64, 1)
    )

    def pivot(k, carry):
        pick = jnp.full((8, CHORD), k, jnp.int32)
        row_re = jnp.broadcast_to(gauss[pl.ds(k, 1), :], (8, CHORD))
        row_im = jnp.broadcast_to(gauss[pl.ds(64 + k, 1), :], (8, CHORD))
        scale = 1.0 / jnp.take_along_axis(row_re, pick, axis=1)
        row_re = row_re * scale
        row_im = row_im * scale
        for block in range(8):
            here, there = pl.ds(8 * block, 8), pl.ds(64 + 8 * block, 8)
            old_re, old_im = gauss[here, :], gauss[there, :]
            col_re = jnp.take_along_axis(old_re, pick, axis=1)
            col_im = jnp.take_along_axis(old_im, pick, axis=1)
            gauss[here, :] = old_re - col_re * row_re + col_im * row_im
            gauss[there, :] = old_im - col_re * row_im - col_im * row_re
        gauss[pl.ds(k, 1), :] = row_re[0:1]
        gauss[pl.ds(64 + k, 1), :] = row_im[0:1]
        return carry

    lax.fori_loop(0, 20, pivot, 0)
    arrived(recv1.at[pl.ds(0, 7)], recv_sem.at[3])

    base = recv1[0, 2:3, :]
    sums = [jnp.zeros((1, CHORD), jnp.float32) for _ in range(3)]
    for j in range(8):
        for part in range(2):
            row = recv1[j, part : part + 1, :]
            blade = recv1[j, 2 + part : 3 + part, :] - base
            for r in range(3):
                sums[r] = sums[r] + jnp.where(blade == float(r), row, 0.0)
    for r in range(3):
        send2[r : r + 1, :] = sums[r]
    send2[3:4, :] = base
    recv2[plane] = send2[...]
    pl.semaphore_wait(known_sem.at[1], XN - 1)
    for dx, dz in planes:
        copy = pltpu.make_async_remote_copy(
            src_ref=send2,
            dst_ref=recv2.at[plane],
            send_sem=send_sem.at[4],
            recv_sem=recv_sem.at[4],
            device_id=plane_device(dx, dz),
            device_id_type=MESH,
        )
        copy.start()

    lax.fori_loop(20, MODES, pivot, 0)
    back_re = pltpu.roll(gauss[0:64, :], 64, 1)
    back_im = pltpu.roll(gauss[64:128, :], 64, 1)
    inverse[0:64, :] = jnp.where(left_half, back_re, -gauss[64:128, :])
    inverse[64:128, :] = jnp.where(left_half, back_im, gauss[0:64, :])

    arrived(recv2.at[pl.ds(0, 31)], recv_sem.at[4])
    everything = recv2[...]
    summed = jnp.sum(everything, axis=0)
    total = summed[0:1] + summed[1:2] + summed[2:3]
    lane1 = lax.broadcasted_iota(jnp.int32, (1, CHORD), 1)
    used = (lane1 < MODES) | ((lane1 >= 64) & (lane1 < 64 + MODES))
    total = jnp.where(used, total * (1.0 / 1024.0), 0.0)
    solved = lax.dot_general(
        jnp.broadcast_to(total, (8, CHORD)), inverse[...], contract,
        precision=HIGHEST, preferred_element_type=jnp.float32,
    )[0:1]
    amplitude = jnp.where(used, solved, 0.0).astype(jnp.bfloat16).astype(jnp.float32)

    def share(part):
        recv3[part, member] = send3[part]
        for dy, dh in group:
            pltpu.make_async_remote_copy(
                src_ref=send3.at[part],
                dst_ref=recv3.at[part, member],
                send_sem=send_sem.at[5 + part],
                recv_sem=recv_sem.at[5 + part],
                device_id=group_device(dy, dh),
                device_id_type=MESH,
            ).start()

    send3[0] = amplitude
    share(0)
    row3 = lax.broadcasted_iota(jnp.int32, (32, 4, CHORD), 1).astype(jnp.float32)
    lane3 = lax.broadcasted_iota(jnp.int32, (32, 4, CHORD), 2).astype(jnp.float32)
    belongs = (everything[:, 3:4, :] + row3 == lane3) & (row3 < 3.0)
    dots = jnp.sum(everything * amplitude, axis=2, keepdims=True)
    send3[1] = jnp.sum(jnp.sum(jnp.where(belongs, dots, 0.0), axis=0), axis=0, keepdims=True)
    share(1)
    counted = jnp.sum(jnp.where(lane3 == 62.0, everything, 0.0), axis=2, keepdims=True)
    counts = jnp.sum(jnp.sum(jnp.where(belongs, counted, 0.0), axis=0), axis=0, keepdims=True)
    counts = jnp.where(lane1 < BLADES, counts * CHORD, 1.0)

    arrived(recv3.at[0, pl.ds(0, 7)], recv_sem.at[5])
    amplitudes = jnp.concatenate([recv3[0, j] for j in range(8)], axis=0)
    both_parts = jnp.concatenate([amplitudes, pltpu.roll(amplitudes, 64, 1)], axis=0)
    both_parts = both_parts[:, 0:64].astype(jnp.bfloat16)
    for s in range(0, OWN, 4):
        lanes = slice(s * CHORD, (s + 4) * CHORD)
        rebuilt = jnp.dot(both_parts, shapes_flat[:, lanes], preferred_element_type=jnp.float32)
        product = jnp.sum(rebuilt * wall[:, lanes].astype(jnp.float32), axis=0, keepdims=True)
        for i in range(4):
            sens_ref[s + i : s + i + 1, :] = product[:, i * CHORD : (i + 1) * CHORD]

    arrived(recv3.at[1, pl.ds(0, 7)], recv_sem.at[6])
    totals = recv3[1, 0]
    for j in range(1, 8):
        totals = totals + recv3[1, j]
    load_ref[...] = totals * lax.rsqrt(counts)

    arrived(halves, send_sem.at[0])
    one_edge = first.at[pl.ds(0, 3), pl.ds(0, 3), pl.ds(0, HARM), :]
    arrived(one_edge, send_sem.at[1])
    arrived(one_edge, send_sem.at[2])
    arrived(recv1.at[pl.ds(0, 7)], send_sem.at[3])
    arrived(recv2.at[pl.ds(0, 31)], send_sem.at[4])
    arrived(recv3.at[0, pl.ds(0, 7)], send_sem.at[5])
    arrived(recv3.at[1, pl.ds(0, 7)], send_sem.at[6])


def per_device(source, mode_shapes, modal_real, modal_imag, harmonic_freq, blade_of_row):
    f32, bf16 = jnp.float32, jnp.bfloat16
    operands = (harmonic_freq, blade_of_row, source, mode_shapes, modal_real, modal_imag)
    hbm = pl.BlockSpec(memory_space=pltpu.HBM)
    vmem = pl.BlockSpec(memory_space=pltpu.VMEM)
    sens, load = pl.pallas_call(
        kernel,
        name="flutter",
        out_shape=(
            pltpu.VMEM((OWN, CHORD), f32),
            pltpu.VMEM((1, CHORD), f32),
        ),
        in_specs=[hbm] * 6,
        out_specs=(vmem, vmem),
        scratch_shapes=[
            pltpu.VMEM((MODES, OWN, CHORD), bf16),
            pltpu.VMEM((64 * OWN, CHORD), f32),
            pltpu.VMEM((64, OWN * CHORD), bf16),
            pltpu.VMEM((LAYERS, SPAN, 16, CHORD), f32),
            pltpu.VMEM((3, SPAN, 16, CHORD), f32),
            pltpu.VMEM((2, SPAN, 16, CHORD), f32),
            pltpu.VMEM((16, OWN * CHORD), bf16),
            pltpu.VMEM((16, OWN * CHORD), bf16),
            pltpu.VMEM((2, MODES, MODES), f32),
            pltpu.VMEM((CHORD, CHORD), f32),
            pltpu.VMEM((CHORD, CHORD), f32),
            pltpu.VMEM((32, CHORD), f32),
            pltpu.VMEM((8, 4, CHORD), f32),
            pltpu.VMEM((8, 4, CHORD), f32),
            pltpu.VMEM((4, CHORD), f32),
            pltpu.VMEM((32, 4, CHORD), f32),
            pltpu.VMEM((2, 1, CHORD), f32),
            pltpu.VMEM((2, 8, 1, CHORD), f32),
            pltpu.SMEM((HARM,), f32),
            pltpu.SMEM((2 * OWN,), jnp.int32),
            pltpu.SemaphoreType.DMA((6,)),
            pltpu.SemaphoreType.DMA((7,)),
            pltpu.SemaphoreType.DMA((7,)),
            pltpu.SemaphoreType.REGULAR((2,)),
        ],
        compiler_params=pltpu.CompilerParams(
            collective_id=0, has_side_effects=True, vmem_limit_bytes=32 * 1024 * 1024
        ),
    )(*(pltpu.with_memory_space_constraint(a, pltpu.HBM) for a in operands))
    return sens, load[0, :BLADES]


def solution(mesh):
    placed = (P("harm", None, "cells", None), P(None, "cells", None), P(), P(), P(), P("cells"))
    return jax.shard_map(
        per_device,
        mesh=mesh,
        in_specs=placed,
        out_specs=(P(("cells", "harm"), None), P()),
        check_vma=False,
    )
```

```python
import itertools

import jax
import jax.numpy as jnp
from jax import lax
from jax.experimental import pallas as pl
from jax.experimental.pallas import tpu as pltpu
from jax.sharding import PartitionSpec as P

BLADES = 24
RELAX = 0.15
DAMPING = 0.5
CENTER = 1.0 - 6.0 * RELAX - RELAX * DAMPING

HARM = 7
MODES = 60
LAYERS = 4
CHORD = 128
OWN = 32
EDGE_ROWS = ((0, 0), (1, 3), (2, 5))
PIVOTS = (8, 14)
SPAN = 38
XN, ZN, YN = 4, 8, 4
MESH = pl.DeviceIdType.MESH
HIGHEST = lax.Precision.HIGHEST


def place():
    cell = lax.axis_index("cells")
    return cell // (ZN * YN), (cell // YN) % ZN, cell % YN, lax.axis_index("harm")


def cell_of(x, z, y):
    return (x * ZN + z) * YN + y


def kernel(
    freq_hbm, blade_hbm, source_ref, shapes_ref, real_ref, imag_ref,
    sens_ref, load_ref,
    edge, edge_in, shapes_raw, shapes_wide, shapes_flat, first, second, third, wall,
    pair, gauss, inverse, packed, send1, recv1, send2, recv2, send3, recv3,
    freq_ref, blade_ref, local_sem, send_sem, recv_sem, known_sem,
):
    x, z, y, h = place()
    cell = lax.axis_index("cells")
    cells = XN * ZN * YN
    colour = lax.rem(x + 2 * y, 4)
    member = 4 * h + colour
    up_cell = lax.rem(cell + 1, cells)
    down_cell = lax.rem(cell + cells - 1, cells)
    mine = jnp.minimum(member, HARM - 1)

    barrier = pltpu.get_barrier_semaphore()

    def device(dx, dz, dy, dh=0):
        to_cell = cell_of(lax.rem(x + dx, XN), lax.rem(z + dz, ZN), lax.rem(y + dy, YN))
        return to_cell, lax.rem(h + dh, 2)

    def hops(step):
        return sum(min(d, n - d) for d, n in zip(step, (XN, ZN, YN)))

    chips = itertools.product(range(XN), range(ZN), range(YN))
    chips = sorted((c for c in chips if any(c)), key=lambda c: -hops(c))
    sources = [(1, 0, 0), (XN - 1, 0, 0), (0, 0, 1)]
    takers = [(XN - 1, 0, 0), (1, 0, 0), (0, 0, YN - 1)]
    takers = [(*c, dh) for c in takers for dh in range(2)] + [(0, 0, 0, 1)]
    near = [(0, 0, 0, 1)]
    near += [(*c, dh) for c in (*sources, (0, 0, YN - 1)) for dh in range(2)]
    near += [(2, 0, 0, 0), (0, 0, 2, 0)] + [(0, dz, 0, 0) for dz in (1, 2, ZN - 2, ZN - 1)]
    edge_cell = jnp.where(h == 0, down_cell, up_cell)
    nearby = [(edge_cell, 0), (edge_cell, 1)] + [device(*step) for step in near]
    for one in nearby:
        pl.semaphore_signal(barrier, inc=1, device_id=one, device_id_type=MESH)

    def arrived(array, sem):
        pltpu.make_async_copy(array, array, sem).wait()

    for c in range(HARM):
        for layer, offset in EDGE_ROWS:
            count = 3 - layer
            for side, station in ((0, 61 + layer), (1, 0)):
                pltpu.make_async_copy(
                    source_ref.at[c, layer, pl.ds(station, count), :],
                    edge.at[side, pl.ds(offset, count), c, :],
                    local_sem.at[6],
                ).start()
    freq_copy = pltpu.make_async_copy(freq_hbm, freq_ref, local_sem.at[4])
    blade_copy = pltpu.make_async_copy(blade_hbm, blade_ref, local_sem.at[5])
    freq_copy.start()
    blade_copy.start()
    pl.semaphore_wait(barrier, len(nearby))

    arrived(edge.at[:, :, pl.ds(0, HARM), :], local_sem.at[6])
    pltpu.make_async_remote_copy(
        src_ref=edge.at[0],
        dst_ref=edge_in.at[h],
        send_sem=send_sem.at[1],
        recv_sem=recv_sem.at[1],
        device_id=(up_cell, 0),
        device_id_type=MESH,
    ).start()
    pltpu.make_async_remote_copy(
        src_ref=edge.at[1],
        dst_ref=edge_in.at[h],
        send_sem=send_sem.at[2],
        recv_sem=recv_sem.at[1],
        device_id=(down_cell, 1),
        device_id_type=MESH,
    ).start()
    for c in range(HARM):
        pltpu.make_async_remote_copy(
            src_ref=source_ref.at[c, :, pl.ds((1 - h) * 29, 35), :],
            dst_ref=first.at[:, pl.ds(3 * h, 35), h * 8 + c, :],
            send_sem=send_sem.at[0],
            recv_sem=recv_sem.at[0],
            device_id=(cell, 1 - h),
            device_id_type=MESH,
        ).start()

    shape_copy = pltpu.make_async_copy(
        shapes_ref.at[:, pl.ds(pl.multiple_of(h * OWN, OWN), OWN), :],
        shapes_raw.at[pl.ds(0, MODES)],
        local_sem.at[1],
    )
    shape_copy.start()
    real_copy = pltpu.make_async_copy(real_ref.at[mine], pair.at[0], local_sem.at[2])
    imag_copy = pltpu.make_async_copy(imag_ref.at[mine], pair.at[1], local_sem.at[3])
    real_copy.start()
    imag_copy.start()
    start = h * 29
    for c in range(HARM):
        pltpu.make_async_copy(
            source_ref.at[c, :, pl.ds(start, 35), :],
            first.at[:, pl.ds(3 - 3 * h, 35), h * 8 + c, :],
            local_sem.at[0],
        ).start()
    blade_copy.wait()
    first_blade = blade_ref[0]
    last_blade = blade_ref[2 * OWN - 1]
    blade_row = h * OWN
    low_count = jnp.float32(0.0)
    for s in range(OWN):
        same = blade_ref[blade_row + s] == first_blade
        low_count = low_count + jnp.where(same, jnp.float32(1.0), jnp.float32(0.0))

    for step in [(0, 2, 0), (0, ZN - 2, 0), (1, 0, 0), (2, 0, 0), (3, 0, 0)]:
        pl.semaphore_signal(
            known_sem.at[0], inc=1, device_id=device(*step), device_id_type=MESH
        )

    shapes_wide[pl.ds(MODES * OWN, 4 * OWN), :] = jnp.zeros((4 * OWN, CHORD), jnp.float32)

    shape_copy.wait()

    def widen(m, carry):
        shapes_wide[pl.ds(pl.multiple_of(m * OWN, OWN), OWN), :] = shapes_raw[m].astype(jnp.float32)
        return carry

    lax.fori_loop(0, MODES, widen, 0, unroll=4)

    def flatten(s, carry):
        rows = shapes_wide[pl.ds(s, 64, stride=OWN), :]
        shapes_flat[:, pl.ds(pl.multiple_of(s * CHORD, CHORD), CHORD)] = rows.astype(jnp.bfloat16)
        return carry

    lax.fori_loop(0, OWN, flatten, 0, unroll=4)

    pl.semaphore_wait(known_sem.at[0], 5)
    flat = [c for c in chips if c[1] == 0]
    for step in flat:
        pl.semaphore_signal(
            known_sem.at[1], inc=1, device_id=device(*step), device_id_type=MESH
        )

    sub = lax.broadcasted_iota(jnp.int32, (16, CHORD), 0)
    lane16 = lax.broadcasted_iota(jnp.int32, (16, CHORD), 1)
    freq_copy.wait()
    coupling = jnp.zeros((16, CHORD), jnp.float32)
    for k in range(HARM):
        value = RELAX * freq_ref[k]
        coupling = jnp.where(sub == k, value, jnp.where(sub == 8 + k, -value, coupling))
    not_last = lane16 < CHORD - 1
    not_first = lane16 > 0

    def relaxed(field, layers, layer, t):
        centre = field[layer, t]
        near = field[layer, t + 1] + field[layer, t - 1]
        near = near + jnp.where(not_last, pltpu.roll(centre, CHORD - 1, 1), 0.0)
        near = near + jnp.where(not_first, pltpu.roll(centre, 1, 1), 0.0)
        if layer + 1 < layers:
            near = near + field[layer + 1, t]
        if layer > 0:
            near = near + field[layer - 1, t]
        partner = jnp.concatenate([centre[8:16], centre[0:8]], axis=0)
        return CENTER * centre + coupling * partner + RELAX * (near + first[layer, t])

    in_use = (sub != 7) & (sub != 15)

    def relax_rows(first_t, second_t, third_t, first_n, second_n, third_n):
        def step_one(i, carry):
            for layer in range(3):
                second[layer, first_t + i] = relaxed(first, 4, layer, first_t + i)
            return carry

        def step_two(i, carry):
            for layer in range(2):
                third[layer, second_t + i] = relaxed(second, 3, layer, second_t + i)
            return carry

        def step_three(i, carry):
            s = third_t - 3 + i
            value = jnp.where(in_use, relaxed(third, 2, 0, third_t + i), 0.0).astype(jnp.bfloat16)
            same = blade_ref[blade_row + s] == first_blade
            weight = jnp.where(same, jnp.float32(1.0), jnp.float32(0.0))
            lanes = pl.ds(pl.multiple_of(s * CHORD, CHORD), CHORD)
            wall[0:16, lanes] = value
            wall[16:32, lanes] = (value.astype(jnp.float32) * weight).astype(jnp.bfloat16)
            return carry

        lax.fori_loop(0, first_n, step_one, 0, unroll=min(first_n, 11))
        lax.fori_loop(0, second_n, step_two, 0, unroll=min(second_n, 16))
        lax.fori_loop(0, third_n, step_three, 0, unroll=True)

    contract = (((1,), (1,)), ((), ()))

    def loads(lanes):
        packed[:, 0:64] += lax.dot_general(
            wall[:, lanes], shapes_flat[:, lanes], contract, preferred_element_type=jnp.float32
        )

    edge_lanes = pl.ds(pl.multiple_of(h * (29 * CHORD), CHORD), 3 * CHORD)
    wall[:, edge_lanes] = jnp.zeros((32, 3 * CHORD), jnp.bfloat16)
    packed[...] = jnp.zeros_like(packed)
    halves = first.at[:, pl.ds(0, 35), pl.ds(0, HARM), :]
    arrived(halves, local_sem.at[0])
    arrived(halves, recv_sem.at[0])
    relax_rows(4 - 3 * h, 4 - 2 * h, 6 - 3 * h, 33, 32, 29)
    loads(pl.ds(0, OWN * CHORD))
    lane = lax.broadcasted_iota(jnp.int32, (64, CHORD), 1)
    left_half = lane < 64
    real_copy.wait()
    imag_copy.wait()
    gauss[...] = jnp.zeros_like(gauss)
    gauss[0:MODES, 0:MODES] = pair[0]
    gauss[64 : 64 + MODES, 0:MODES] = pair[1]
    both = gauss[0:64, :] + pltpu.roll(gauss[64:128, :], 64, 1)
    system = jnp.concatenate([both, jnp.zeros_like(both)], axis=0)
    adjoint = jnp.transpose(system)
    gram = jnp.dot(adjoint, system, precision=HIGHEST, preferred_element_type=jnp.float32)
    top, low = gram[0:64], gram[64:128]
    gauss[0:64, :] = jnp.where(
        left_half, top + pltpu.roll(low, 64, 1), pltpu.roll(adjoint[0:64], 64, 1)
    )
    gauss[64:128, :] = jnp.where(
        left_half, pltpu.roll(top, 64, 1) - low, -pltpu.roll(adjoint[64:128], 64, 1)
    )

    def pivot(k, carry):
        pick = jnp.full((8, CHORD), k, jnp.int32)
        row_re = jnp.broadcast_to(gauss[pl.ds(k, 1), :], (8, CHORD))
        row_im = jnp.broadcast_to(gauss[pl.ds(64 + k, 1), :], (8, CHORD))
        scale = 1.0 / jnp.take_along_axis(row_re, pick, axis=1)
        row_re = row_re * scale
        row_im = row_im * scale
        for block in range(8):
            here, there = pl.ds(8 * block, 8), pl.ds(64 + 8 * block, 8)
            old_re, old_im = gauss[here, :], gauss[there, :]
            col_re = jnp.take_along_axis(old_re, pick, axis=1)
            col_im = jnp.take_along_axis(old_im, pick, axis=1)
            gauss[here, :] = old_re - col_re * row_re + col_im * row_im
            gauss[there, :] = old_im - col_re * row_im - col_im * row_re
        gauss[pl.ds(k, 1), :] = row_re[0:1]
        gauss[pl.ds(64 + k, 1), :] = row_im[0:1]
        return carry

    lax.fori_loop(0, PIVOTS[0], pivot, 0)
    arrived(edge_in, recv_sem.at[1])
    for core in range(2):
        for layer, offset in EDGE_ROWS:
            for i in range(3 - layer):
                t = i + layer * (1 - h) + 35 * h
                first[layer, t, 8 * core : 8 * core + 8, :] = edge_in[core, offset + i]
    relax_rows(1 + 33 * h, 2 + 31 * h, 3 + 29 * h, 3, 3, 3)
    loads(edge_lanes)

    lane8 = lax.broadcasted_iota(jnp.int32, (8, CHORD), 1)
    whole = packed[0:8, :] + pltpu.roll(packed[8:16, :], 64, 1)
    lower = packed[16:24, :] + pltpu.roll(packed[24:32, :], 64, 1)
    upper = whole - lower
    lower = jnp.where(lane8 == 62, low_count, lower)
    upper = jnp.where(lane8 == 62, OWN - low_count, upper)
    for core in range(2):
        send1[core, 0:4, :] = lower[4 * core : 4 * core + 4]
        send1[core, 4:8, :] = upper[4 * core : 4 * core + 4]
    pltpu.make_async_remote_copy(
        src_ref=send1.at[1 - h],
        dst_ref=recv1,
        send_sem=send_sem.at[3],
        recv_sem=recv_sem.at[3],
        device_id=(cell, 1 - h),
        device_id_type=MESH,
    ).start()

    lax.fori_loop(PIVOTS[0], PIVOTS[1], pivot, 0)
    arrived(recv1, recv_sem.at[3])

    lane1 = lax.broadcasted_iota(jnp.int32, (1, CHORD), 1)
    low_id = jnp.full((1, CHORD), first_blade, jnp.int32).astype(jnp.float32)
    high_id = jnp.full((1, CHORD), last_blade, jnp.int32).astype(jnp.float32)
    chip_rows = send1[h] + recv1[...]
    send2[0] = jnp.where(lane1 == 63, low_id, chip_rows[0:4])
    send2[1] = jnp.where(lane1 == 63, high_id, chip_rows[4:8])
    two_rows = pl.ds(2 * cell, 2)
    recv2[pl.ds(2 * cell, 1), :] = send2[0, pl.ds(colour, 1), :]
    recv2[pl.ds(2 * cell + 1, 1), :] = send2[1, pl.ds(colour, 1), :]
    pl.semaphore_wait(known_sem.at[1], len(flat))
    for step in chips:
        pltpu.make_async_remote_copy(
            src_ref=send2.at[:, lax.rem(colour + step[0] + 2 * step[2], 4), :],
            dst_ref=recv2.at[two_rows],
            send_sem=send_sem.at[4],
            recv_sem=recv_sem.at[4],
            device_id=device(*step),
            device_id_type=MESH,
        ).start()

    lax.fori_loop(PIVOTS[1], MODES, pivot, 0)
    back_re = pltpu.roll(gauss[0:64, :], 64, 1)
    back_im = pltpu.roll(gauss[64:128, :], 64, 1)
    inverse[0:64, :] = jnp.where(left_half, back_re, -gauss[64:128, :])
    inverse[64:128, :] = jnp.where(left_half, back_im, gauss[0:64, :])

    arrived(recv2.at[pl.ds(0, 254)], recv_sem.at[4])
    everything = recv2[...]
    total = jnp.sum(everything, axis=0, keepdims=True)
    used = (lane1 < MODES) | ((lane1 >= 64) & (lane1 < 64 + MODES))
    total = jnp.where(used, total * (1.0 / 1024.0), 0.0)
    solved = lax.dot_general(
        jnp.broadcast_to(total, (8, CHORD)), inverse[...], contract,
        precision=HIGHEST, preferred_element_type=jnp.float32,
    )[0:1]
    amplitude = jnp.where(used, solved, 0.0).astype(jnp.bfloat16).astype(jnp.float32)

    def share(part):
        recv3[part, pl.ds(member, 1), :] = send3[part]
        for step in takers:
            pltpu.make_async_remote_copy(
                src_ref=send3.at[part],
                dst_ref=recv3.at[part, pl.ds(member, 1)],
                send_sem=send_sem.at[5 + part],
                recv_sem=recv_sem.at[5 + part],
                device_id=device(*step),
                device_id_type=MESH,
            ).start()

    send3[0] = amplitude
    share(0)
    lane2 = lax.broadcasted_iota(jnp.int32, (256, CHORD), 1).astype(jnp.float32)

    def along(values):
        return jnp.sum(values, axis=1, keepdims=True)

    belongs = along(jnp.where(lane2 == 63.0, everything, 0.0)) == lane2

    def by_blade(values):
        return jnp.sum(jnp.where(belongs, values, 0.0), axis=0, keepdims=True)

    send3[1] = by_blade(along(everything * amplitude))
    share(1)
    counts = by_blade(along(jnp.where(lane2 == 62.0, everything, 0.0)))
    counts = jnp.where(lane1 < BLADES, counts * CHORD, 1.0)

    arrived(recv3.at[0, pl.ds(0, 7)], recv_sem.at[5])
    amplitudes = recv3[0]
    both_parts = jnp.concatenate([amplitudes, pltpu.roll(amplitudes, 64, 1)], axis=0)
    both_parts = both_parts[:, 0:64].astype(jnp.bfloat16)
    for s in range(0, OWN, 4):
        lanes = slice(s * CHORD, (s + 4) * CHORD)
        rebuilt = jnp.dot(both_parts, shapes_flat[:, lanes], preferred_element_type=jnp.float32)
        product = jnp.sum(rebuilt * wall[0:16, lanes].astype(jnp.float32), axis=0, keepdims=True)
        for i in range(4):
            sens_ref[s + i : s + i + 1, :] = product[:, i * CHORD : (i + 1) * CHORD]

    arrived(recv3.at[1, pl.ds(0, 7)], recv_sem.at[6])
    totals = jnp.sum(recv3[1], axis=0, keepdims=True)
    load_ref[...] = totals * lax.rsqrt(counts)

    arrived(halves, send_sem.at[0])
    arrived(edge.at[0], send_sem.at[1])
    arrived(edge.at[1], send_sem.at[2])
    arrived(recv1, send_sem.at[3])
    arrived(recv2.at[pl.ds(0, 254)], send_sem.at[4])
    arrived(recv3.at[0, pl.ds(0, 7)], send_sem.at[5])
    arrived(recv3.at[1, pl.ds(0, 7)], send_sem.at[6])


def per_device(source, mode_shapes, modal_real, modal_imag, harmonic_freq, blade_of_row):
    f32, bf16 = jnp.float32, jnp.bfloat16
    operands = (harmonic_freq, blade_of_row, source, mode_shapes, modal_real, modal_imag)
    hbm = pl.BlockSpec(memory_space=pltpu.HBM)
    vmem = pl.BlockSpec(memory_space=pltpu.VMEM)
    sens, load = pl.pallas_call(
        kernel,
        name="flutter",
        out_shape=(
            pltpu.VMEM((OWN, CHORD), f32),
            pltpu.VMEM((1, CHORD), f32),
        ),
        in_specs=[hbm] * 6,
        out_specs=(vmem, vmem),
        scratch_shapes=[
            pltpu.VMEM((2, 6, 8, CHORD), f32),
            pltpu.VMEM((2, 6, 8, CHORD), f32),
            pltpu.VMEM((MODES, OWN, CHORD), bf16),
            pltpu.VMEM((64 * OWN, CHORD), f32),
            pltpu.VMEM((64, OWN * CHORD), bf16),
            pltpu.VMEM((LAYERS, SPAN, 16, CHORD), f32),
            pltpu.VMEM((3, SPAN, 16, CHORD), f32),
            pltpu.VMEM((2, SPAN, 16, CHORD), f32),
            pltpu.VMEM((32, OWN * CHORD), bf16),
            pltpu.VMEM((2, MODES, MODES), f32),
            pltpu.VMEM((CHORD, CHORD), f32),
            pltpu.VMEM((CHORD, CHORD), f32),
            pltpu.VMEM((32, CHORD), f32),
            pltpu.VMEM((2, 8, CHORD), f32),
            pltpu.VMEM((8, CHORD), f32),
            pltpu.VMEM((2, 4, CHORD), f32),
            pltpu.VMEM((256, CHORD), f32),
            pltpu.VMEM((2, 1, CHORD), f32),
            pltpu.VMEM((2, 8, CHORD), f32),
            pltpu.SMEM((HARM,), f32),
            pltpu.SMEM((2 * OWN,), jnp.int32),
            pltpu.SemaphoreType.DMA((7,)),
            pltpu.SemaphoreType.DMA((7,)),
            pltpu.SemaphoreType.DMA((7,)),
            pltpu.SemaphoreType.REGULAR((2,)),
        ],
        compiler_params=pltpu.CompilerParams(
            collective_id=0, has_side_effects=True, vmem_limit_bytes=32 * 1024 * 1024
        ),
    )(*(pltpu.with_memory_space_constraint(a, pltpu.HBM) for a in operands))
    return sens, load[0, :BLADES]


def solution(mesh):
    placed = (P("harm", None, "cells", None), P(None, "cells", None), P(), P(), P(), P("cells"))
    return jax.shard_map(
        per_device,
        mesh=mesh,
        in_specs=placed,
        out_specs=(P(("cells", "harm"), None), P()),
        check_vma=False,
    )
```

```python
import itertools

import jax
import jax.numpy as jnp
from jax import lax
from jax.experimental import pallas as pl
from jax.experimental.pallas import tpu as pltpu
from jax.sharding import PartitionSpec as P

BLADES = 24
RELAX = 0.15
DAMPING = 0.5
CENTER = 1.0 - 6.0 * RELAX - RELAX * DAMPING

HARM = 7
MODES = 60
LAYERS = 4
CHORD = 128
OWN = 32
EDGE_ROWS = ((0, 0), (1, 3), (2, 5))
SPAN = 38
XN, ZN, YN = 4, 8, 4
MESH = pl.DeviceIdType.MESH
HIGHEST = lax.Precision.HIGHEST


def place():
    cell = lax.axis_index("cells")
    return cell // (ZN * YN), (cell // YN) % ZN, cell % YN, lax.axis_index("harm")


def cell_of(x, z, y):
    return (x * ZN + z) * YN + y


def kernel(
    freq_hbm, blade_hbm, source_ref, shapes_ref, real_ref, imag_ref,
    sens_ref, load_ref,
    edge, edge_in, shapes_raw, shapes_wide, shapes_flat, first, second, third, wall,
    pair, gauss, inverse, packed, send1, recv1, send2, recv2, send3, recv3,
    freq_ref, blade_ref, local_sem, send_sem, recv_sem, known_sem,
):
    x, z, y, h = place()
    cell = lax.axis_index("cells")
    cells = XN * ZN * YN
    colour = lax.rem(x + 2 * y, 4)
    member = 4 * h + colour
    up_cell = lax.rem(cell + 1, cells)
    down_cell = lax.rem(cell + cells - 1, cells)
    mine = jnp.minimum(member, HARM - 1)

    barrier = pltpu.get_barrier_semaphore()

    def device(dx, dz, dy, dh=0):
        to_cell = cell_of(lax.rem(x + dx, XN), lax.rem(z + dz, ZN), lax.rem(y + dy, YN))
        return to_cell, lax.rem(h + dh, 2)

    def hops(step):
        return sum(min(d, n - d) for d, n in zip(step, (XN, ZN, YN)))

    chips = itertools.product(range(XN), range(ZN), range(YN))
    chips = sorted((c for c in chips if any(c)), key=lambda c: -hops(c))
    sources = [(1, 0, 0), (XN - 1, 0, 0), (0, 0, 1)]
    takers = [(XN - 1, 0, 0), (1, 0, 0), (0, 0, YN - 1)]
    takers = [(*c, dh) for c in takers for dh in range(2)] + [(0, 0, 0, 1)]
    near = [(0, 0, 0, 1)]
    near += [(*c, dh) for c in (*sources, (0, 0, YN - 1)) for dh in range(2)]
    near += [(2, 0, 0, 0), (0, 0, 2, 0)] + [(0, dz, 0, 0) for dz in (1, 2, ZN - 2, ZN - 1)]
    edge_cell = jnp.where(h == 0, down_cell, up_cell)
    nearby = [(edge_cell, 0), (edge_cell, 1)] + [device(*step) for step in near]
    for one in nearby:
        pl.semaphore_signal(barrier, inc=1, device_id=one, device_id_type=MESH)

    def arrived(array, sem):
        pltpu.make_async_copy(array, array, sem).wait()

    for c in range(HARM):
        for layer, offset in EDGE_ROWS:
            count = 3 - layer
            for side, station in ((0, 61 + layer), (1, 0)):
                pltpu.make_async_copy(
                    source_ref.at[c, layer, pl.ds(station, count), :],
                    edge.at[side, pl.ds(offset, count), c, :],
                    local_sem.at[6],
                ).start()
    freq_copy = pltpu.make_async_copy(freq_hbm, freq_ref, local_sem.at[4])
    blade_copy = pltpu.make_async_copy(blade_hbm, blade_ref, local_sem.at[5])
    freq_copy.start()
    blade_copy.start()
    pl.semaphore_wait(barrier, len(nearby))

    arrived(edge.at[:, :, pl.ds(0, HARM), :], local_sem.at[6])
    pltpu.make_async_remote_copy(
        src_ref=edge.at[0],
        dst_ref=edge_in.at[h],
        send_sem=send_sem.at[1],
        recv_sem=recv_sem.at[1],
        device_id=(up_cell, 0),
        device_id_type=MESH,
    ).start()
    pltpu.make_async_remote_copy(
        src_ref=edge.at[1],
        dst_ref=edge_in.at[h],
        send_sem=send_sem.at[2],
        recv_sem=recv_sem.at[1],
        device_id=(down_cell, 1),
        device_id_type=MESH,
    ).start()
    for c in range(HARM):
        pltpu.make_async_remote_copy(
            src_ref=source_ref.at[c, :, pl.ds((1 - h) * 29, 35), :],
            dst_ref=first.at[:, pl.ds(3 * h, 35), h * 8 + c, :],
            send_sem=send_sem.at[0],
            recv_sem=recv_sem.at[0],
            device_id=(cell, 1 - h),
            device_id_type=MESH,
        ).start()

    shape_copy = pltpu.make_async_copy(
        shapes_ref.at[:, pl.ds(pl.multiple_of(h * OWN, OWN), OWN), :],
        shapes_raw.at[pl.ds(0, MODES)],
        local_sem.at[1],
    )
    shape_copy.start()
    real_copy = pltpu.make_async_copy(real_ref.at[mine], pair.at[0], local_sem.at[2])
    imag_copy = pltpu.make_async_copy(imag_ref.at[mine], pair.at[1], local_sem.at[3])
    real_copy.start()
    imag_copy.start()
    start = h * 29
    for c in range(HARM):
        pltpu.make_async_copy(
            source_ref.at[c, :, pl.ds(start, 35), :],
            first.at[:, pl.ds(3 - 3 * h, 35), h * 8 + c, :],
            local_sem.at[0],
        ).start()
    blade_copy.wait()
    first_blade = blade_ref[0]
    last_blade = blade_ref[2 * OWN - 1]
    blade_row = h * OWN
    low_count = jnp.float32(0.0)
    for s in range(OWN):
        same = blade_ref[blade_row + s] == first_blade
        low_count = low_count + jnp.where(same, jnp.float32(1.0), jnp.float32(0.0))

    for step in [(0, 2, 0), (0, ZN - 2, 0), (1, 0, 0), (2, 0, 0), (3, 0, 0)]:
        pl.semaphore_signal(
            known_sem.at[0], inc=1, device_id=device(*step), device_id_type=MESH
        )

    shapes_wide[pl.ds(MODES * OWN, 4 * OWN), :] = jnp.zeros((4 * OWN, CHORD), jnp.float32)

    shape_copy.wait()

    def widen(m, carry):
        shapes_wide[pl.ds(pl.multiple_of(m * OWN, OWN), OWN), :] = shapes_raw[m].astype(jnp.float32)
        return carry

    lax.fori_loop(0, MODES, widen, 0, unroll=4)

    def flatten(s, carry):
        rows = shapes_wide[pl.ds(s, 64, stride=OWN), :]
        shapes_flat[:, pl.ds(pl.multiple_of(s * CHORD, CHORD), CHORD)] = rows.astype(jnp.bfloat16)
        return carry

    lax.fori_loop(0, OWN, flatten, 0, unroll=4)

    pl.semaphore_wait(known_sem.at[0], 5)
    flat = [c for c in chips if c[1] == 0]
    for step in flat:
        pl.semaphore_signal(
            known_sem.at[1], inc=1, device_id=device(*step), device_id_type=MESH
        )

    sub = lax.broadcasted_iota(jnp.int32, (16, CHORD), 0)
    lane16 = lax.broadcasted_iota(jnp.int32, (16, CHORD), 1)
    freq_copy.wait()
    coupling = jnp.zeros((16, CHORD), jnp.float32)
    for k in range(HARM):
        value = RELAX * freq_ref[k]
        coupling = jnp.where(sub == k, value, jnp.where(sub == 8 + k, -value, coupling))
    not_last = lane16 < CHORD - 1
    not_first = lane16 > 0

    def relaxed(field, layers, layer, t):
        centre = field[layer, t]
        near = field[layer, t + 1] + field[layer, t - 1]
        near = near + jnp.where(not_last, pltpu.roll(centre, CHORD - 1, 1), 0.0)
        near = near + jnp.where(not_first, pltpu.roll(centre, 1, 1), 0.0)
        if layer + 1 < layers:
            near = near + field[layer + 1, t]
        if layer > 0:
            near = near + field[layer - 1, t]
        partner = jnp.concatenate([centre[8:16], centre[0:8]], axis=0)
        return CENTER * centre + coupling * partner + RELAX * (near + first[layer, t])

    in_use = (sub != 7) & (sub != 15)

    def relax_rows(first_t, second_t, third_t, first_n, second_n, third_n):
        def step_one(i, carry):
            for layer in range(3):
                second[layer, first_t + i] = relaxed(first, 4, layer, first_t + i)
            return carry

        def step_two(i, carry):
            for layer in range(2):
                third[layer, second_t + i] = relaxed(second, 3, layer, second_t + i)
            return carry

        def step_three(i, carry):
            s = third_t - 3 + i
            value = jnp.where(in_use, relaxed(third, 2, 0, third_t + i), 0.0).astype(jnp.bfloat16)
            same = blade_ref[blade_row + s] == first_blade
            weight = jnp.where(same, jnp.float32(1.0), jnp.float32(0.0))
            lanes = pl.ds(pl.multiple_of(s * CHORD, CHORD), CHORD)
            wall[0:16, lanes] = value
            wall[16:32, lanes] = (value.astype(jnp.float32) * weight).astype(jnp.bfloat16)
            return carry

        lax.fori_loop(0, first_n, step_one, 0, unroll=min(first_n, 11))
        lax.fori_loop(0, second_n, step_two, 0, unroll=min(second_n, 16))
        lax.fori_loop(0, third_n, step_three, 0, unroll=True)

    contract = (((1,), (1,)), ((), ()))

    def loads(lanes):
        packed[:, 0:64] += lax.dot_general(
            wall[:, lanes], shapes_flat[:, lanes], contract, preferred_element_type=jnp.float32
        )

    edge_lanes = pl.ds(pl.multiple_of(h * (29 * CHORD), CHORD), 3 * CHORD)
    wall[:, edge_lanes] = jnp.zeros((32, 3 * CHORD), jnp.bfloat16)
    packed[...] = jnp.zeros_like(packed)
    halves = first.at[:, pl.ds(0, 35), pl.ds(0, HARM), :]
    arrived(halves, local_sem.at[0])
    arrived(halves, recv_sem.at[0])
    relax_rows(4 - 3 * h, 4 - 2 * h, 6 - 3 * h, 33, 32, 29)
    loads(pl.ds(0, OWN * CHORD))
    arrived(edge_in, recv_sem.at[1])
    for core in range(2):
        for layer, offset in EDGE_ROWS:
            for i in range(3 - layer):
                t = i + layer * (1 - h) + 35 * h
                first[layer, t, 8 * core : 8 * core + 8, :] = edge_in[core, offset + i]
    relax_rows(1 + 33 * h, 2 + 31 * h, 3 + 29 * h, 3, 3, 3)
    loads(edge_lanes)

    lane8 = lax.broadcasted_iota(jnp.int32, (8, CHORD), 1)
    whole = packed[0:8, :] + pltpu.roll(packed[8:16, :], 64, 1)
    lower = packed[16:24, :] + pltpu.roll(packed[24:32, :], 64, 1)
    upper = whole - lower
    lower = jnp.where(lane8 == 62, low_count, lower)
    upper = jnp.where(lane8 == 62, OWN - low_count, upper)
    for core in range(2):
        send1[core, 0:4, :] = lower[4 * core : 4 * core + 4]
        send1[core, 4:8, :] = upper[4 * core : 4 * core + 4]
    pltpu.make_async_remote_copy(
        src_ref=send1.at[1 - h],
        dst_ref=recv1,
        send_sem=send_sem.at[3],
        recv_sem=recv_sem.at[3],
        device_id=(cell, 1 - h),
        device_id_type=MESH,
    ).start()

    arrived(recv1, recv_sem.at[3])

    lane1 = lax.broadcasted_iota(jnp.int32, (1, CHORD), 1)
    low_id = jnp.full((1, CHORD), first_blade, jnp.int32).astype(jnp.float32)
    high_id = jnp.full((1, CHORD), last_blade, jnp.int32).astype(jnp.float32)
    chip_rows = send1[h] + recv1[...]
    send2[0] = jnp.where(lane1 == 63, low_id, chip_rows[0:4])
    send2[1] = jnp.where(lane1 == 63, high_id, chip_rows[4:8])
    two_rows = pl.ds(2 * cell, 2)
    recv2[pl.ds(2 * cell, 1), :] = send2[0, pl.ds(colour, 1), :]
    recv2[pl.ds(2 * cell + 1, 1), :] = send2[1, pl.ds(colour, 1), :]
    pl.semaphore_wait(known_sem.at[1], len(flat))
    for step in chips:
        pltpu.make_async_remote_copy(
            src_ref=send2.at[:, lax.rem(colour + step[0] + 2 * step[2], 4), :],
            dst_ref=recv2.at[two_rows],
            send_sem=send_sem.at[4],
            recv_sem=recv_sem.at[4],
            device_id=device(*step),
            device_id_type=MESH,
        ).start()

    lane = lax.broadcasted_iota(jnp.int32, (64, CHORD), 1)
    left_half = lane < 64
    real_copy.wait()
    imag_copy.wait()
    gauss[...] = jnp.zeros_like(gauss)
    gauss[0:MODES, 0:MODES] = pair[0]
    gauss[64 : 64 + MODES, 0:MODES] = pair[1]
    both = gauss[0:64, :] + pltpu.roll(gauss[64:128, :], 64, 1)
    system = jnp.concatenate([both, jnp.zeros_like(both)], axis=0)
    adjoint = jnp.transpose(system)
    gram = jnp.dot(adjoint, system, precision=HIGHEST, preferred_element_type=jnp.float32)
    top, low = gram[0:64], gram[64:128]
    gauss[0:64, :] = jnp.where(
        left_half, top + pltpu.roll(low, 64, 1), pltpu.roll(adjoint[0:64], 64, 1)
    )
    gauss[64:128, :] = jnp.where(
        left_half, pltpu.roll(top, 64, 1) - low, -pltpu.roll(adjoint[64:128], 64, 1)
    )

    def pivot(k, carry):
        pick = jnp.full((8, CHORD), k, jnp.int32)
        row_re = jnp.broadcast_to(gauss[pl.ds(k, 1), :], (8, CHORD))
        row_im = jnp.broadcast_to(gauss[pl.ds(64 + k, 1), :], (8, CHORD))
        scale = 1.0 / jnp.take_along_axis(row_re, pick, axis=1)
        row_re = row_re * scale
        row_im = row_im * scale
        for block in range(8):
            here, there = pl.ds(8 * block, 8), pl.ds(64 + 8 * block, 8)
            old_re, old_im = gauss[here, :], gauss[there, :]
            col_re = jnp.take_along_axis(old_re, pick, axis=1)
            col_im = jnp.take_along_axis(old_im, pick, axis=1)
            gauss[here, :] = old_re - col_re * row_re + col_im * row_im
            gauss[there, :] = old_im - col_re * row_im - col_im * row_re
        gauss[pl.ds(k, 1), :] = row_re[0:1]
        gauss[pl.ds(64 + k, 1), :] = row_im[0:1]
        return carry

    lax.fori_loop(0, MODES, pivot, 0)
    back_re = pltpu.roll(gauss[0:64, :], 64, 1)
    back_im = pltpu.roll(gauss[64:128, :], 64, 1)
    inverse[0:64, :] = jnp.where(left_half, back_re, -gauss[64:128, :])
    inverse[64:128, :] = jnp.where(left_half, back_im, gauss[0:64, :])

    arrived(recv2.at[pl.ds(0, 254)], recv_sem.at[4])
    everything = recv2[...]
    total = jnp.sum(everything, axis=0, keepdims=True)
    used = (lane1 < MODES) | ((lane1 >= 64) & (lane1 < 64 + MODES))
    total = jnp.where(used, total * (1.0 / 1024.0), 0.0)
    solved = lax.dot_general(
        jnp.broadcast_to(total, (8, CHORD)), inverse[...], contract,
        precision=HIGHEST, preferred_element_type=jnp.float32,
    )[0:1]
    amplitude = jnp.where(used, solved, 0.0).astype(jnp.bfloat16).astype(jnp.float32)

    def share(part):
        recv3[part, pl.ds(member, 1), :] = send3[part]
        for step in takers:
            pltpu.make_async_remote_copy(
                src_ref=send3.at[part],
                dst_ref=recv3.at[part, pl.ds(member, 1)],
                send_sem=send_sem.at[5 + part],
                recv_sem=recv_sem.at[5 + part],
                device_id=device(*step),
                device_id_type=MESH,
            ).start()

    send3[0] = amplitude
    share(0)
    lane2 = lax.broadcasted_iota(jnp.int32, (256, CHORD), 1).astype(jnp.float32)

    def along(values):
        return jnp.sum(values, axis=1, keepdims=True)

    belongs = along(jnp.where(lane2 == 63.0, everything, 0.0)) == lane2

    def by_blade(values):
        return jnp.sum(jnp.where(belongs, values, 0.0), axis=0, keepdims=True)

    send3[1] = by_blade(along(everything * amplitude))
    share(1)
    counts = by_blade(along(jnp.where(lane2 == 62.0, everything, 0.0)))
    counts = jnp.where(lane1 < BLADES, counts * CHORD, 1.0)

    arrived(recv3.at[0, pl.ds(0, 7)], recv_sem.at[5])
    amplitudes = recv3[0]
    both_parts = jnp.concatenate([amplitudes, pltpu.roll(amplitudes, 64, 1)], axis=0)
    both_parts = both_parts[:, 0:64].astype(jnp.bfloat16)
    for s in range(0, OWN, 4):
        lanes = slice(s * CHORD, (s + 4) * CHORD)
        rebuilt = jnp.dot(both_parts, shapes_flat[:, lanes], preferred_element_type=jnp.float32)
        product = jnp.sum(rebuilt * wall[0:16, lanes].astype(jnp.float32), axis=0, keepdims=True)
        for i in range(4):
            sens_ref[s + i : s + i + 1, :] = product[:, i * CHORD : (i + 1) * CHORD]

    arrived(recv3.at[1, pl.ds(0, 7)], recv_sem.at[6])
    totals = jnp.sum(recv3[1], axis=0, keepdims=True)
    load_ref[...] = totals * lax.rsqrt(counts)

    arrived(halves, send_sem.at[0])
    arrived(edge.at[0], send_sem.at[1])
    arrived(edge.at[1], send_sem.at[2])
    arrived(recv1, send_sem.at[3])
    arrived(recv2.at[pl.ds(0, 254)], send_sem.at[4])
    arrived(recv3.at[0, pl.ds(0, 7)], send_sem.at[5])
    arrived(recv3.at[1, pl.ds(0, 7)], send_sem.at[6])


def per_device(source, mode_shapes, modal_real, modal_imag, harmonic_freq, blade_of_row):
    f32, bf16 = jnp.float32, jnp.bfloat16
    operands = (harmonic_freq, blade_of_row, source, mode_shapes, modal_real, modal_imag)
    hbm = pl.BlockSpec(memory_space=pltpu.HBM)
    vmem = pl.BlockSpec(memory_space=pltpu.VMEM)
    sens, load = pl.pallas_call(
        kernel,
        name="flutter",
        out_shape=(
            pltpu.VMEM((OWN, CHORD), f32),
            pltpu.VMEM((1, CHORD), f32),
        ),
        in_specs=[hbm] * 6,
        out_specs=(vmem, vmem),
        scratch_shapes=[
            pltpu.VMEM((2, 6, 8, CHORD), f32),
            pltpu.VMEM((2, 6, 8, CHORD), f32),
            pltpu.VMEM((MODES, OWN, CHORD), bf16),
            pltpu.VMEM((64 * OWN, CHORD), f32),
            pltpu.VMEM((64, OWN * CHORD), bf16),
            pltpu.VMEM((LAYERS, SPAN, 16, CHORD), f32),
            pltpu.VMEM((3, SPAN, 16, CHORD), f32),
            pltpu.VMEM((2, SPAN, 16, CHORD), f32),
            pltpu.VMEM((32, OWN * CHORD), bf16),
            pltpu.VMEM((2, MODES, MODES), f32),
            pltpu.VMEM((CHORD, CHORD), f32),
            pltpu.VMEM((CHORD, CHORD), f32),
            pltpu.VMEM((32, CHORD), f32),
            pltpu.VMEM((2, 8, CHORD), f32),
            pltpu.VMEM((8, CHORD), f32),
            pltpu.VMEM((2, 4, CHORD), f32),
            pltpu.VMEM((256, CHORD), f32),
            pltpu.VMEM((2, 1, CHORD), f32),
            pltpu.VMEM((2, 8, CHORD), f32),
            pltpu.SMEM((HARM,), f32),
            pltpu.SMEM((2 * OWN,), jnp.int32),
            pltpu.SemaphoreType.DMA((7,)),
            pltpu.SemaphoreType.DMA((7,)),
            pltpu.SemaphoreType.DMA((7,)),
            pltpu.SemaphoreType.REGULAR((2,)),
        ],
        compiler_params=pltpu.CompilerParams(
            collective_id=0, has_side_effects=True, vmem_limit_bytes=32 * 1024 * 1024
        ),
    )(*(pltpu.with_memory_space_constraint(a, pltpu.HBM) for a in operands))
    return sens, load[0, :BLADES]


def solution(mesh):
    placed = (P("harm", None, "cells", None), P(None, "cells", None), P(), P(), P(), P("cells"))
    return jax.shard_map(
        per_device,
        mesh=mesh,
        in_specs=placed,
        out_specs=(P(("cells", "harm"), None), P()),
        check_vma=False,
    )
```

```python
import itertools

import jax
import jax.numpy as jnp
from jax import lax
from jax.experimental import pallas as pl
from jax.experimental.pallas import tpu as pltpu
from jax.sharding import PartitionSpec as P

BLADES = 24
RELAX = 0.15
DAMPING = 0.5
CENTER = 1.0 - 6.0 * RELAX - RELAX * DAMPING

HARM = 7
MODES = 60
LAYERS = 4
CHORD = 128
OWN = 32
EDGE_ROWS = ((0, 0), (1, 3), (2, 5))
SPAN = 38
XN, ZN, YN = 4, 8, 4
MESH = pl.DeviceIdType.MESH
HIGHEST = lax.Precision.HIGHEST


def place():
    cell = lax.axis_index("cells")
    return cell // (ZN * YN), (cell // YN) % ZN, cell % YN, lax.axis_index("harm")


def cell_of(x, z, y):
    return (x * ZN + z) * YN + y


def kernel(
    freq_hbm, blade_hbm, source_ref, shapes_ref, real_ref, imag_ref,
    sens_ref, load_ref,
    edge, edge_in, shapes_raw, shapes_wide, shapes_flat, first, second, third, wall,
    pair, gauss, inverse, packed, send1, recv1, send2, recv2, send3, recv3,
    freq_ref, blade_ref, local_sem, send_sem, recv_sem, known_sem,
):
    x, z, y, h = place()
    cell = lax.axis_index("cells")
    cells = XN * ZN * YN
    colour = lax.rem(x + 2 * y, 4)
    member = 4 * h + colour
    up_cell = lax.rem(cell + 1, cells)
    down_cell = lax.rem(cell + cells - 1, cells)
    mine = jnp.minimum(member, HARM - 1)

    barrier = pltpu.get_barrier_semaphore()

    def device(dx, dz, dy, dh=0):
        to_cell = cell_of(lax.rem(x + dx, XN), lax.rem(z + dz, ZN), lax.rem(y + dy, YN))
        return to_cell, lax.rem(h + dh, 2)

    def hops(step):
        return sum(min(d, n - d) for d, n in zip(step, (XN, ZN, YN)))

    chips = itertools.product(range(XN), range(ZN), range(YN))
    chips = sorted((c for c in chips if any(c)), key=lambda c: -hops(c))
    sources = [(1, 0, 0), (XN - 1, 0, 0), (0, 0, 1)]
    takers = [(XN - 1, 0, 0), (1, 0, 0), (0, 0, YN - 1)]
    takers = [(*c, dh) for c in takers for dh in range(2)] + [(0, 0, 0, 1)]
    near = [(0, 0, 0, 1)]
    near += [(*c, dh) for c in (*sources, (0, 0, YN - 1)) for dh in range(2)]
    near += [(2, 0, 0, 0), (0, 0, 2, 0)] + [(0, dz, 0, 0) for dz in (1, 2, ZN - 2, ZN - 1)]
    edge_cell = jnp.where(h == 0, down_cell, up_cell)
    nearby = [(edge_cell, 0), (edge_cell, 1)] + [device(*step) for step in near]
    for one in nearby:
        pl.semaphore_signal(barrier, inc=1, device_id=one, device_id_type=MESH)

    def arrived(array, sem):
        pltpu.make_async_copy(array, array, sem).wait()

    for c in range(HARM):
        for layer, offset in EDGE_ROWS:
            count = 3 - layer
            for side, station in ((0, 61 + layer), (1, 0)):
                pltpu.make_async_copy(
                    source_ref.at[c, layer, pl.ds(station, count), :],
                    edge.at[side, pl.ds(offset, count), c, :],
                    local_sem.at[6],
                ).start()
    freq_copy = pltpu.make_async_copy(freq_hbm, freq_ref, local_sem.at[4])
    blade_copy = pltpu.make_async_copy(blade_hbm, blade_ref, local_sem.at[5])
    freq_copy.start()
    blade_copy.start()
    pl.semaphore_wait(barrier, len(nearby))

    arrived(edge.at[:, :, pl.ds(0, HARM), :], local_sem.at[6])
    pltpu.make_async_remote_copy(
        src_ref=edge.at[0],
        dst_ref=edge_in.at[h],
        send_sem=send_sem.at[1],
        recv_sem=recv_sem.at[1],
        device_id=(up_cell, 0),
        device_id_type=MESH,
    ).start()
    pltpu.make_async_remote_copy(
        src_ref=edge.at[1],
        dst_ref=edge_in.at[h],
        send_sem=send_sem.at[2],
        recv_sem=recv_sem.at[1],
        device_id=(down_cell, 1),
        device_id_type=MESH,
    ).start()
    for c in range(HARM):
        pltpu.make_async_remote_copy(
            src_ref=source_ref.at[c, :, pl.ds((1 - h) * 29, 35), :],
            dst_ref=first.at[:, pl.ds(3 * h, 35), h * 8 + c, :],
            send_sem=send_sem.at[0],
            recv_sem=recv_sem.at[0],
            device_id=(cell, 1 - h),
            device_id_type=MESH,
        ).start()

    shape_copy = pltpu.make_async_copy(
        shapes_ref.at[:, pl.ds(pl.multiple_of(h * OWN, OWN), OWN), :],
        shapes_raw.at[pl.ds(0, MODES)],
        local_sem.at[1],
    )
    shape_copy.start()
    real_copy = pltpu.make_async_copy(real_ref.at[mine], pair.at[0], local_sem.at[2])
    imag_copy = pltpu.make_async_copy(imag_ref.at[mine], pair.at[1], local_sem.at[3])
    real_copy.start()
    imag_copy.start()
    start = h * 29
    for c in range(HARM):
        pltpu.make_async_copy(
            source_ref.at[c, :, pl.ds(start, 35), :],
            first.at[:, pl.ds(3 - 3 * h, 35), h * 8 + c, :],
            local_sem.at[0],
        ).start()
    blade_copy.wait()
    first_blade = blade_ref[0]
    last_blade = blade_ref[2 * OWN - 1]
    blade_row = h * OWN
    low_count = jnp.float32(0.0)
    for s in range(OWN):
        same = blade_ref[blade_row + s] == first_blade
        low_count = low_count + jnp.where(same, jnp.float32(1.0), jnp.float32(0.0))

    for step in [(0, 2, 0), (0, ZN - 2, 0), (1, 0, 0), (2, 0, 0), (3, 0, 0)]:
        pl.semaphore_signal(
            known_sem.at[0], inc=1, device_id=device(*step), device_id_type=MESH
        )

    shapes_wide[pl.ds(MODES * OWN, 4 * OWN), :] = jnp.zeros((4 * OWN, CHORD), jnp.float32)

    shape_copy.wait()

    def widen(m, carry):
        shapes_wide[pl.ds(pl.multiple_of(m * OWN, OWN), OWN), :] = shapes_raw[m].astype(jnp.float32)
        return carry

    lax.fori_loop(0, MODES, widen, 0, unroll=4)

    def flatten(s, carry):
        rows = shapes_wide[pl.ds(s, 64, stride=OWN), :]
        shapes_flat[:, pl.ds(pl.multiple_of(s * CHORD, CHORD), CHORD)] = rows.astype(jnp.bfloat16)
        return carry

    lax.fori_loop(0, OWN, flatten, 0, unroll=4)

    pl.semaphore_wait(known_sem.at[0], 5)
    flat = [c for c in chips if c[1] == 0]
    for step in flat:
        pl.semaphore_signal(
            known_sem.at[1], inc=1, device_id=device(*step), device_id_type=MESH
        )

    sub = lax.broadcasted_iota(jnp.int32, (16, CHORD), 0)
    lane16 = lax.broadcasted_iota(jnp.int32, (16, CHORD), 1)
    freq_copy.wait()
    coupling = jnp.zeros((16, CHORD), jnp.float32)
    for k in range(HARM):
        value = RELAX * freq_ref[k]
        coupling = jnp.where(sub == k, value, jnp.where(sub == 8 + k, -value, coupling))
    not_last = lane16 < CHORD - 1
    not_first = lane16 > 0

    def relaxed(field, layers, layer, t):
        centre = field[layer, t]
        near = field[layer, t + 1] + field[layer, t - 1]
        near = near + jnp.where(not_last, pltpu.roll(centre, CHORD - 1, 1), 0.0)
        near = near + jnp.where(not_first, pltpu.roll(centre, 1, 1), 0.0)
        if layer + 1 < layers:
            near = near + field[layer + 1, t]
        if layer > 0:
            near = near + field[layer - 1, t]
        partner = jnp.concatenate([centre[8:16], centre[0:8]], axis=0)
        return CENTER * centre + coupling * partner + RELAX * (near + first[layer, t])

    in_use = (sub != 7) & (sub != 15)

    def relax_rows(first_t, second_t, third_t, first_n, second_n, third_n):
        def step_one(i, carry):
            for layer in range(3):
                second[layer, first_t + i] = relaxed(first, 4, layer, first_t + i)
            return carry

        def step_two(i, carry):
            for layer in range(2):
                third[layer, second_t + i] = relaxed(second, 3, layer, second_t + i)
            return carry

        def step_three(i, carry):
            s = third_t - 3 + i
            value = jnp.where(in_use, relaxed(third, 2, 0, third_t + i), 0.0).astype(jnp.bfloat16)
            same = blade_ref[blade_row + s] == first_blade
            weight = jnp.where(same, jnp.float32(1.0), jnp.float32(0.0))
            lanes = pl.ds(pl.multiple_of(s * CHORD, CHORD), CHORD)
            wall[0:16, lanes] = value
            wall[16:32, lanes] = (value.astype(jnp.float32) * weight).astype(jnp.bfloat16)
            return carry

        if first_n:
            lax.fori_loop(0, first_n, step_one, 0, unroll=min(first_n, 11))
            lax.fori_loop(0, second_n, step_two, 0, unroll=min(second_n, 16))
        lax.fori_loop(0, third_n, step_three, 0, unroll=True)

    contract = (((1,), (1,)), ((), ()))

    def loads(lanes):
        packed[:, 0:64] += lax.dot_general(
            wall[:, lanes], shapes_flat[:, lanes], contract, preferred_element_type=jnp.float32
        )

    edge_lanes = pl.ds(pl.multiple_of(h * (29 * CHORD), CHORD), 3 * CHORD)
    wall[:, edge_lanes] = jnp.zeros((32, 3 * CHORD), jnp.bfloat16)
    packed[...] = jnp.zeros_like(packed)
    halves = first.at[:, pl.ds(0, 35), pl.ds(0, HARM), :]
    arrived(halves, local_sem.at[0])
    arrived(halves, recv_sem.at[0])
    relax_rows(4 - 3 * h, 4 - 2 * h, 6 - 3 * h, 33, 32, 29)
    loads(pl.ds(0, OWN * CHORD))
    arrived(edge_in, recv_sem.at[1])
    for core in range(2):
        for layer, offset in EDGE_ROWS:
            for i in range(3 - layer):
                t = i + layer * (1 - h) + 35 * h
                first[layer, t, 8 * core : 8 * core + 8, :] = edge_in[core, offset + i]
    for layer, steps in ((0, (1, 2, 3)), (1, (2, 3)), (2, (3,))):
        for step in steps:
            t = step + h * (SPAN - 1 - 2 * step)
            second[layer, t] = relaxed(first, 4, layer, t)
    for layer, steps in ((0, (2, 3, 4)), (1, (3, 4))):
        for step in steps:
            t = step + h * (SPAN - 1 - 2 * step)
            third[layer, t] = relaxed(second, 3, layer, t)
    relax_rows(0, 0, 3 + 29 * h, 0, 0, 3)
    loads(edge_lanes)

    lane8 = lax.broadcasted_iota(jnp.int32, (8, CHORD), 1)
    whole = packed[0:8, :] + pltpu.roll(packed[8:16, :], 64, 1)
    lower = packed[16:24, :] + pltpu.roll(packed[24:32, :], 64, 1)
    upper = whole - lower
    lower = jnp.where(lane8 == 62, low_count, lower)
    upper = jnp.where(lane8 == 62, OWN - low_count, upper)
    for core in range(2):
        send1[core, 0:4, :] = lower[4 * core : 4 * core + 4]
        send1[core, 4:8, :] = upper[4 * core : 4 * core + 4]
    pltpu.make_async_remote_copy(
        src_ref=send1.at[1 - h],
        dst_ref=recv1,
        send_sem=send_sem.at[3],
        recv_sem=recv_sem.at[3],
        device_id=(cell, 1 - h),
        device_id_type=MESH,
    ).start()

    arrived(recv1, recv_sem.at[3])

    lane1 = lax.broadcasted_iota(jnp.int32, (1, CHORD), 1)
    low_id = jnp.full((1, CHORD), first_blade, jnp.int32).astype(jnp.float32)
    high_id = jnp.full((1, CHORD), last_blade, jnp.int32).astype(jnp.float32)
    chip_rows = send1[h] + recv1[...]
    send2[0] = jnp.where(lane1 == 63, low_id, chip_rows[0:4])
    send2[1] = jnp.where(lane1 == 63, high_id, chip_rows[4:8])
    two_rows = pl.ds(2 * cell, 2)
    recv2[pl.ds(2 * cell, 1), :] = send2[0, pl.ds(colour, 1), :]
    recv2[pl.ds(2 * cell + 1, 1), :] = send2[1, pl.ds(colour, 1), :]
    pl.semaphore_wait(known_sem.at[1], len(flat))
    for step in chips:
        pltpu.make_async_remote_copy(
            src_ref=send2.at[:, lax.rem(colour + step[0] + 2 * step[2], 4), :],
            dst_ref=recv2.at[two_rows],
            send_sem=send_sem.at[4],
            recv_sem=recv_sem.at[4],
            device_id=device(*step),
            device_id_type=MESH,
        ).start()

    lane = lax.broadcasted_iota(jnp.int32, (64, CHORD), 1)
    left_half = lane < 64
    real_copy.wait()
    imag_copy.wait()
    gauss[...] = jnp.zeros_like(gauss)
    gauss[0:MODES, 0:MODES] = pair[0]
    gauss[64 : 64 + MODES, 0:MODES] = pair[1]
    both = gauss[0:64, :] + pltpu.roll(gauss[64:128, :], 64, 1)
    system = jnp.concatenate([both, jnp.zeros_like(both)], axis=0)
    adjoint = jnp.transpose(system)
    gram = jnp.dot(adjoint, system, precision=HIGHEST, preferred_element_type=jnp.float32)
    top, low = gram[0:64], gram[64:128]
    gauss[0:64, :] = jnp.where(
        left_half, top + pltpu.roll(low, 64, 1), pltpu.roll(adjoint[0:64], 64, 1)
    )
    gauss[64:128, :] = jnp.where(
        left_half, pltpu.roll(top, 64, 1) - low, -pltpu.roll(adjoint[64:128], 64, 1)
    )

    def pivot(k, carry):
        pick = jnp.full((8, CHORD), k, jnp.int32)
        row_re = jnp.broadcast_to(gauss[pl.ds(k, 1), :], (8, CHORD))
        row_im = jnp.broadcast_to(gauss[pl.ds(64 + k, 1), :], (8, CHORD))
        scale = 1.0 / jnp.take_along_axis(row_re, pick, axis=1)
        row_re = row_re * scale
        row_im = row_im * scale
        for block in range(8):
            here, there = pl.ds(8 * block, 8), pl.ds(64 + 8 * block, 8)
            old_re, old_im = gauss[here, :], gauss[there, :]
            col_re = jnp.take_along_axis(old_re, pick, axis=1)
            col_im = jnp.take_along_axis(old_im, pick, axis=1)
            gauss[here, :] = old_re - col_re * row_re + col_im * row_im
            gauss[there, :] = old_im - col_re * row_im - col_im * row_re
        gauss[pl.ds(k, 1), :] = row_re[0:1]
        gauss[pl.ds(64 + k, 1), :] = row_im[0:1]
        return carry

    lax.fori_loop(0, MODES, pivot, 0)
    back_re = pltpu.roll(gauss[0:64, :], 64, 1)
    back_im = pltpu.roll(gauss[64:128, :], 64, 1)
    inverse[0:64, :] = jnp.where(left_half, back_re, -gauss[64:128, :])
    inverse[64:128, :] = jnp.where(left_half, back_im, gauss[0:64, :])

    arrived(recv2.at[pl.ds(0, 254)], recv_sem.at[4])
    everything = recv2[...]
    total = jnp.sum(everything, axis=0, keepdims=True)
    used = (lane1 < MODES) | ((lane1 >= 64) & (lane1 < 64 + MODES))
    total = jnp.where(used, total * (1.0 / 1024.0), 0.0)
    solved = lax.dot_general(
        jnp.broadcast_to(total, (8, CHORD)), inverse[...], contract,
        precision=HIGHEST, preferred_element_type=jnp.float32,
    )[0:1]
    amplitude = jnp.where(used, solved, 0.0).astype(jnp.bfloat16).astype(jnp.float32)

    def share(part):
        recv3[part, pl.ds(member, 1), :] = send3[part]
        for step in takers:
            pltpu.make_async_remote_copy(
                src_ref=send3.at[part],
                dst_ref=recv3.at[part, pl.ds(member, 1)],
                send_sem=send_sem.at[5 + part],
                recv_sem=recv_sem.at[5 + part],
                device_id=device(*step),
                device_id_type=MESH,
            ).start()

    send3[0] = amplitude
    share(0)
    lane2 = lax.broadcasted_iota(jnp.int32, (256, CHORD), 1).astype(jnp.float32)

    def along(values):
        return jnp.sum(values, axis=1, keepdims=True)

    belongs = along(jnp.where(lane2 == 63.0, everything, 0.0)) == lane2

    def by_blade(values):
        return jnp.sum(jnp.where(belongs, values, 0.0), axis=0, keepdims=True)

    send3[1] = by_blade(along(everything * amplitude))
    share(1)
    counts = by_blade(along(jnp.where(lane2 == 62.0, everything, 0.0)))
    counts = jnp.where(lane1 < BLADES, counts * CHORD, 1.0)

    arrived(recv3.at[0, pl.ds(0, 7)], recv_sem.at[5])
    amplitudes = recv3[0]
    both_parts = jnp.concatenate([amplitudes, pltpu.roll(amplitudes, 64, 1)], axis=0)
    both_parts = both_parts[:, 0:64].astype(jnp.bfloat16)
    for s in range(0, OWN, 4):
        lanes = slice(s * CHORD, (s + 4) * CHORD)
        rebuilt = jnp.dot(both_parts, shapes_flat[:, lanes], preferred_element_type=jnp.float32)
        product = jnp.sum(rebuilt * wall[0:16, lanes].astype(jnp.float32), axis=0, keepdims=True)
        for i in range(4):
            sens_ref[s + i : s + i + 1, :] = product[:, i * CHORD : (i + 1) * CHORD]

    arrived(recv3.at[1, pl.ds(0, 7)], recv_sem.at[6])
    totals = jnp.sum(recv3[1], axis=0, keepdims=True)
    load_ref[...] = totals * lax.rsqrt(counts)

    arrived(halves, send_sem.at[0])
    arrived(edge.at[0], send_sem.at[1])
    arrived(edge.at[1], send_sem.at[2])
    arrived(recv1, send_sem.at[3])
    arrived(recv2.at[pl.ds(0, 254)], send_sem.at[4])
    arrived(recv3.at[0, pl.ds(0, 7)], send_sem.at[5])
    arrived(recv3.at[1, pl.ds(0, 7)], send_sem.at[6])


def per_device(source, mode_shapes, modal_real, modal_imag, harmonic_freq, blade_of_row):
    f32, bf16 = jnp.float32, jnp.bfloat16
    operands = (harmonic_freq, blade_of_row, source, mode_shapes, modal_real, modal_imag)
    hbm = pl.BlockSpec(memory_space=pltpu.HBM)
    vmem = pl.BlockSpec(memory_space=pltpu.VMEM)
    sens, load = pl.pallas_call(
        kernel,
        name="flutter",
        out_shape=(
            pltpu.VMEM((OWN, CHORD), f32),
            pltpu.VMEM((1, CHORD), f32),
        ),
        in_specs=[hbm] * 6,
        out_specs=(vmem, vmem),
        scratch_shapes=[
            pltpu.VMEM((2, 6, 8, CHORD), f32),
            pltpu.VMEM((2, 6, 8, CHORD), f32),
            pltpu.VMEM((MODES, OWN, CHORD), bf16),
            pltpu.VMEM((64 * OWN, CHORD), f32),
            pltpu.VMEM((64, OWN * CHORD), bf16),
            pltpu.VMEM((LAYERS, SPAN, 16, CHORD), f32),
            pltpu.VMEM((3, SPAN, 16, CHORD), f32),
            pltpu.VMEM((2, SPAN, 16, CHORD), f32),
            pltpu.VMEM((32, OWN * CHORD), bf16),
            pltpu.VMEM((2, MODES, MODES), f32),
            pltpu.VMEM((CHORD, CHORD), f32),
            pltpu.VMEM((CHORD, CHORD), f32),
            pltpu.VMEM((32, CHORD), f32),
            pltpu.VMEM((2, 8, CHORD), f32),
            pltpu.VMEM((8, CHORD), f32),
            pltpu.VMEM((2, 4, CHORD), f32),
            pltpu.VMEM((256, CHORD), f32),
            pltpu.VMEM((2, 1, CHORD), f32),
            pltpu.VMEM((2, 8, CHORD), f32),
            pltpu.SMEM((HARM,), f32),
            pltpu.SMEM((2 * OWN,), jnp.int32),
            pltpu.SemaphoreType.DMA((7,)),
            pltpu.SemaphoreType.DMA((7,)),
            pltpu.SemaphoreType.DMA((7,)),
            pltpu.SemaphoreType.REGULAR((2,)),
        ],
        compiler_params=pltpu.CompilerParams(
            collective_id=0, has_side_effects=True, vmem_limit_bytes=32 * 1024 * 1024
        ),
    )(*(pltpu.with_memory_space_constraint(a, pltpu.HBM) for a in operands))
    return sens, load[0, :BLADES]


def solution(mesh):
    placed = (P("harm", None, "cells", None), P(None, "cells", None), P(), P(), P(), P("cells"))
    return jax.shard_map(
        per_device,
        mesh=mesh,
        in_specs=placed,
        out_specs=(P(("cells", "harm"), None), P()),
        check_vma=False,
    )
```
